32 devices in a mesh: seq: 8 (over z, x), tp: 4 (over y, core).
Axes of the slice: x: 2, y: 2, z: 4, core: 2. Of those that a mesh axis runs over, the one named last changes fastest.
Arguments:
- mr_qkv: bfloat16 [8192, 3, 4096], P('seq', None, 'tp'), may hold values from -6 to 6
- residual_in: bfloat16 [8192, 4096], P('seq', 'tp'), may hold values from -6 to 6
- mr_short: float32 [7, 3, 4096], P(None, None, 'tp'), may hold values from -2 to 2
- mr_filter: bfloat16 [128, 4096], P(None, 'tp'), may hold values from -0.5 to 0.5
- mr_out: bfloat16 [4096, 4096], P('seq', 'tp'), may hold values from -0.09375 to 0.09375
- norm_gain: float32 [4096], replicated, may hold values from 0.5 to 1.5
- lr_in: bfloat16 [4096, 3, 4096], P('seq', None, 'tp'), may hold values from -0.09375 to 0.09375
- lr_short: float32 [7, 3, 4096], P(None, None, 'tp'), may hold values from -2 to 2
- lr_rate: float32 [16, 4096], P(None, 'tp'), may hold values from 0 to 1, as said below
- lr_residue: float32 [16, 4096], P(None, 'tp'), may hold values from -1.5 to 1.5
Outputs:
- stream: bfloat16 [8192, 4096], P('seq', 'tp')
- lr_gated: bfloat16 [8192, 4096], P('seq', 'tp')
The draws below stay inside these ranges and needn't reach their ends.
Inputs may be any that keep to these rules, and one draw needn't show every extreme that they name: `lr_rate`: every rate is positive.
All inputs are finite; a program needn't handle non-finite values.
Results may differ from the reference program's by a relative error of at most 0.014.
Values may be sent and summed in bfloat16 or wider, within the bound.
No kernel may reach another device: no remote copies, remote signals or barrier semaphores. Data moves between devices by JAX's collectives and lax.ppermute only.
A program may use at most 192 MiB of HBM per device.

```python
import math
import jax
import jax.numpy as jnp
from jax import lax

D = 4096
SHORT = 7
MR_LEN = 128
STATE = 16
TOKENS = 8192
N_TP = 4


def draw_lr_rate(key, part):
    first, second, third = jax.random.split(key, 3)
    shape = (STATE, D)
    slow = jnp.exp(jax.random.uniform(first, shape, jnp.float32, math.log(0.2 / LENGTH_ALIAS(TOKENS)), math.log(2.0 / LENGTH_ALIAS(TOKENS))))
    fast = jnp.exp(jax.random.uniform(second, shape, jnp.float32, math.log(2.0 / LENGTH_ALIAS(TOKENS)), math.log(1.0 / 30.0)))
    pick = jax.random.uniform(third, shape, jnp.float32) < 0.5
    return jnp.where(pick, fast, slow)


def LENGTH_ALIAS(count):
    return float(count)


def level_of(stream_key, extent, cuts, low, largest):
    level = 1.0
    for dim, shards_of in cuts:
        steps = jax.random.uniform(jax.random.fold_in(jax.random.fold_in(stream_key, 6), dim), (shards_of,), jnp.float32, low / len(cuts), largest / len(cuts))
        level = level * jnp.repeat(jnp.exp(steps), extent[dim] // shards_of).reshape((-1,) + (1,) * (len(extent) - 1 - dim))
    return level


def gaussian(key, shape, scale, bound, cuts=(), held_as=jnp.bfloat16):
    result = jax.random.normal(key, shape, jnp.float32) * scale
    if len(cuts) > 0:
        result = level_of(key, shape, cuts, -0.22, 0.18) * result
    return jnp.clip(result, min=-bound, max=bound).astype(held_as)


def setup_inputs(seed: int = 0) -> dict:
    key_of = jax.random.split(jax.random.key(seed), 11)
    return {
        "mr_qkv": gaussian(key_of[0], (TOKENS, 3, D), 1.0, 6.0, ((0, 8), (2, 4))),
        "residual_in": gaussian(key_of[1], (TOKENS, D), 1.0, 6.0, ((0, 8), (1, 4))),
        "mr_short": gaussian(key_of[2], (SHORT, 3, D), SHORT ** -0.5, 2.0, ((2, 4),), jnp.float32),
        "mr_filter": gaussian(key_of[3], (MR_LEN, D), MR_LEN ** -0.5, 0.5, ((1, 4),)),
        "mr_out": gaussian(key_of[4], (D, D), D ** -0.5, 0.09375, ((0, 8), (1, 4))),
        "norm_gain": jnp.clip(1.0 + 0.1 * jax.random.normal(key_of[5], (D,), jnp.float32), 0.5, 1.5),
        "lr_in": gaussian(key_of[6], (D, 3, D), D ** -0.5, 0.09375, ((0, 8), (2, 4))),
        "lr_short": gaussian(key_of[7], (SHORT, 3, D), SHORT ** -0.5, 2.0, ((2, 4),), jnp.float32),
        "lr_rate": draw_lr_rate(jax.random.fold_in(key_of[10], 71), 0),
        "lr_residue": gaussian(key_of[9], (STATE, D), STATE ** -0.5, 1.5, ((1, 4),), jnp.float32),
    }


norm_eps = 1e-06
block_rows = 64
stripe_rows = 512

def featurize(extended, taps, row_count):
    total = jnp.zeros((row_count,) + extended.shape[1:], jnp.float32)
    width = taps.shape[0]
    for tap_index in range(width):
        begin = width - 1 - tap_index
        total = total + taps[tap_index] * extended[begin:begin + row_count].astype(jnp.float32)
    return total

def depthwise(extended, filters):
    width = filters.shape[0]
    row_count = extended.shape[0] - width + 1

    def add_tap(tap_index, total):
        begin = (width - 1 - tap_index).astype(jnp.int32)
        piece = lax.dynamic_slice_in_dim(extended, begin, row_count, 0).astype(jnp.float32)
        weight = lax.dynamic_index_in_dim(filters, tap_index.astype(jnp.int32), 0, False).astype(jnp.float32)
        return total + weight[None] * piece
    start = jnp.zeros((row_count, extended.shape[1]), jnp.float32)
    return lax.fori_loop(0, width, add_tap, start)

def lr_tables(rate, residue):
    coef = residue * jnp.sqrt(2.0 * rate)
    lags = jnp.arange(block_rows).astype(jnp.float32)
    filter_lags = lax.optimization_barrier(jnp.sum(coef[None] * jnp.exp(-rate[None] * lags[:, None, None]), axis=1))
    places = jnp.arange(block_rows, dtype=jnp.int32)
    spread = places[:, None] - places[None, :]
    toeplitz = jnp.where((spread >= 0)[:, :, None], jnp.take(filter_lags, jnp.maximum(spread, 0), axis=0), 0.0)
    into_state = jnp.exp(-rate[None] * (block_rows - 1.0 - lags)[:, None, None])
    from_state = coef[None] * jnp.exp(-rate[None] * (lags + 1.0)[:, None, None])
    step_decay = jnp.exp(-rate * block_rows)
    return (toeplitz, into_state, from_state, step_decay)

def long_conv(values, rate, residue):
    toeplitz, into_state, from_state, step_decay = lr_tables(rate, residue)
    length = values.shape[0]
    group = values.shape[1]
    blocks = values.reshape(length // block_rows, block_rows, group)
    high = lax.Precision.HIGHEST

    def advance(carried, block_vals):
        inside = jnp.einsum('ijc,jc->ic', toeplitz, block_vals, precision=high)
        inside = inside + jnp.einsum('inc,nc->ic', from_state, carried, precision=high)
        carried = step_decay * carried + jnp.einsum('jnc,jc->nc', into_state, block_vals, precision=high)
        return (carried, inside)
    start_state = jnp.zeros((rate.shape[0], group), jnp.float32)
    final_state, outputs = lax.scan(advance, start_state, blocks)
    return outputs.reshape(length, group)

def reference(mr_qkv, residual_in, mr_short, mr_filter, mr_out, norm_gain, lr_in, lr_short, lr_rate, lr_residue):
    length = mr_qkv.shape[0]
    group = D // N_TP

    def mr_block(index):
        begin = index * group
        qkv_part = lax.dynamic_slice_in_dim(mr_qkv, begin, group, 2)
        taps = lax.dynamic_slice_in_dim(mr_short, begin, group, 2)
        filters = lax.dynamic_slice_in_dim(mr_filter, begin, group, 1)
        padded = jnp.pad(qkv_part, ((SHORT - 1, 0), (0, 0), (0, 0)))
        featured = featurize(padded, taps, length)
        product = (featured[:, 1] * featured[:, 2]).astype(jnp.bfloat16)
        medium = depthwise(jnp.pad(product, ((MR_LEN - 1, 0), (0, 0))), filters)
        return (featured[:, 0] * medium).astype(jnp.bfloat16)
    gated = lax.map(mr_block, jnp.arange(N_TP, dtype=jnp.int32))
    gated = gated.transpose(1, 0, 2).reshape(length, D)
    stripes = length // stripe_rows

    def stream_stripe(pair):
        gated_rows, resid_rows = pair
        projected = jnp.dot(gated_rows, mr_out, preferred_element_type=jnp.float32)
        stream_rows = (resid_rows.astype(jnp.float32) + projected).astype(jnp.bfloat16)
        values = stream_rows.astype(jnp.float32)
        scale = lax.rsqrt(lax.optimization_barrier(jnp.mean(values * values, axis=1)) + norm_eps)
        normed_rows = (values * scale[:, None] * norm_gain).astype(jnp.bfloat16)
        return (stream_rows, normed_rows)
    stream, features = lax.map(stream_stripe, (gated.reshape(stripes, stripe_rows, D), residual_in.reshape(stripes, stripe_rows, D)))
    stream = stream.reshape(length, D)
    features = features.reshape(length, D)

    def lr_block(index):
        begin = index * group
        weights = lax.dynamic_slice_in_dim(lr_in, begin, group, 2).reshape(D, 3 * group)
        qkv_part = jnp.dot(features, weights, preferred_element_type=jnp.float32).astype(jnp.bfloat16).reshape(length, 3, group)
        taps = lax.dynamic_slice_in_dim(lr_short, begin, group, 2)
        rate = lax.dynamic_slice_in_dim(lr_rate, begin, group, 1)
        residue = lax.dynamic_slice_in_dim(lr_residue, begin, group, 1)
        padded = jnp.pad(qkv_part, ((SHORT - 1, 0), (0, 0), (0, 0)))
        featured = featurize(padded, taps, length)
        product = (featured[:, 1] * featured[:, 2]).astype(jnp.bfloat16)
        conv = long_conv(product.astype(jnp.float32), rate, residue)
        return (featured[:, 0] * conv).astype(jnp.bfloat16)
    lr_out = lax.map(lr_block, jnp.arange(N_TP, dtype=jnp.int32))
    lr_out = lr_out.transpose(1, 0, 2).reshape(length, D)
    return (stream, lr_out)
```

```python
import functools

import jax
import jax.numpy as jnp
from jax import lax
from jax.experimental import pallas as pl
from jax.experimental.pallas import tpu as pltpu
from jax.sharding import PartitionSpec as P

norm_eps = 1e-06
LANES = 128
SUBS = 8
MR_HALO = 144
LR_HALO = 16
CHUNK = 256
STEP = 8
TILE = 16
MIB = 1024 * 1024


def ring_order(count):
    wide = 4 if count % 16 == 0 else 2
    high = count // wide
    order = [z * wide for z in range(high)]
    for turn, z in enumerate(reversed(range(high))):
        cells = range(1, wide) if turn % 2 == 0 else range(wide - 1, 0, -1)
        order += [z * wide + x for x in cells]
    return order


def featurize(ref, weights, first, sub):
    width = len(weights)
    window = [
        ref[pl.ds(first - (width - 1) + i, SUBS, stride=sub), :] for i in range(STEP + width - 1)
    ]
    out = []
    for i in range(STEP):
        total = weights[0] * window[i + width - 1]
        for j in range(1, width):
            total = total + weights[j] * window[i + width - 1 - j]
        out.append(total)
    return out


def spread(row):
    return jnp.broadcast_to(row, (SUBS, row.shape[-1]))


def mr_kernel(halo_ref, x_ref, short_ref, filter_ref, out_ref, xf, ue, qs, of, ff):
    rows = x_ref.shape[1]
    sub = rows // SUBS
    taps = short_ref.shape[1]
    length = filter_ref.shape[0]
    for g in range(3):
        xf[g, :MR_HALO, :] = halo_ref[g].astype(jnp.float32)
        xf[g, MR_HALO:, :] = x_ref[g].astype(jnp.float32)
    ff[...] = filter_ref[...].astype(jnp.float32)
    weights = [[spread(short_ref[g, pl.ds(j, 1), :]) for j in range(taps)] for g in range(3)]

    def products(step, _):
        first = MR_HALO - sub + step * STEP
        keys = featurize(xf.at[1], weights[1], first, sub)
        values = featurize(xf.at[2], weights[2], first, sub)
        for i in range(STEP):
            ue[step * STEP + i] = (keys[i] * values[i]).astype(jnp.bfloat16).astype(jnp.float32)
        return 0

    lax.fori_loop(0, 2 * sub // STEP, products, 0)

    def queries(step, _):
        found = featurize(xf.at[0], weights[0], MR_HALO + step * STEP, sub)
        for i in range(STEP):
            qs[step * STEP + i] = found[i]
        return 0

    lax.fori_loop(0, sub // STEP, queries, 0)

    def conv(tile, _):
        base = tile * TILE

        def taps_of(part, acc):
            acc = list(acc)
            start = sub + base - part * TILE - (TILE - 1)
            window = [ue[start + m] for m in range(2 * TILE - 1)]
            for j in range(TILE):
                weight = spread(ff[pl.ds(part * TILE + j, 1), :])
                for i in range(TILE):
                    acc[i] = acc[i] + weight * window[i - j + TILE - 1]
            return tuple(acc)

        zero = jnp.zeros((SUBS, LANES), jnp.float32)
        acc = lax.fori_loop(0, length // TILE, taps_of, (zero,) * TILE)
        for i in range(TILE):
            of[pl.ds(base + i, SUBS, stride=sub), :] = acc[i] * qs[base + i]
        return 0

    lax.fori_loop(0, sub // TILE, conv, 0)
    out_ref[...] = of[...].astype(jnp.bfloat16)


def mr_operator(halo, x, short, filters, first, count):
    rows = x.shape[1]
    sub = rows // SUBS
    skip = first // LANES
    return pl.pallas_call(
        mr_kernel,
        grid=(count // LANES,),
        out_shape=jax.ShapeDtypeStruct((rows, count), jnp.bfloat16),
        in_specs=[
            pl.BlockSpec((3, MR_HALO, LANES), lambda i: (0, 0, i + skip)),
            pl.BlockSpec((3, rows, LANES), lambda i: (0, 0, i + skip)),
            pl.BlockSpec((3, short.shape[1], LANES), lambda i: (0, 0, i + skip)),
            pl.BlockSpec((filters.shape[0], LANES), lambda i: (0, i + skip)),
        ],
        out_specs=pl.BlockSpec((rows, LANES), lambda i: (0, i)),
        scratch_shapes=[
            pltpu.VMEM((3, MR_HALO + rows, LANES), jnp.float32),
            pltpu.VMEM((2 * sub, SUBS, LANES), jnp.float32),
            pltpu.VMEM((sub, SUBS, LANES), jnp.float32),
            pltpu.VMEM((rows, LANES), jnp.float32),
            pltpu.VMEM((filters.shape[0], LANES), jnp.float32),
        ],
        compiler_params=pltpu.CompilerParams(vmem_limit_bytes=24 * MIB),
        cost_estimate=pl.CostEstimate(
            flops=rows * count * 340, bytes_accessed=rows * count * 10, transcendentals=0
        ),
        name="mr_operator",
    )(halo, x, short, filters)


def project(cols_ref, a_ref, blocks, pick):
    total = None
    for k, block in enumerate(blocks):
        w = pick(block)
        cols = a_ref[:, pl.ds(pl.multiple_of(cols_ref[k], LANES), w.shape[0])]
        part = jnp.dot(cols, w, preferred_element_type=jnp.float32)
        total = part if total is None else total + part
    return total


def stream_kernel(n_pieces, n_blocks, cols_ref, resid_ref, *refs):
    pieces = refs[:n_pieces]
    blocks = refs[n_pieces : n_pieces + n_blocks]
    out_ref, gated, sems = refs[n_pieces + n_blocks :]
    copies = []
    at = 0
    for i, piece in enumerate(pieces):
        width = piece.shape[1]
        copies.append(pltpu.make_async_copy(piece, gated.at[:, pl.ds(at, width)], sems.at[i]))
        at += width
    for copy in copies:
        copy.start()
    out_ref[:LR_HALO, :] = jnp.zeros((LR_HALO, out_ref.shape[1]), out_ref.dtype)
    for copy in copies:
        copy.wait()

    def tile(i, _):
        lanes = pl.ds(pl.multiple_of(i * CHUNK, CHUNK), CHUNK)
        projected = project(cols_ref, gated, blocks, lambda b: b[:, lanes])
        total = resid_ref[:, lanes].astype(jnp.float32) + projected
        out_ref[LR_HALO:, lanes] = total.astype(jnp.bfloat16)
        return 0

    lax.fori_loop(0, out_ref.shape[1] // CHUNK, tile, 0)


def stream_rows(cols, resid, pieces, blocks):
    rows, channels = resid.shape
    depth = sum(p.shape[1] for p in pieces)
    vmem = pl.BlockSpec(memory_space=pltpu.VMEM)
    return pl.pallas_call(
        functools.partial(stream_kernel, len(pieces), len(blocks)),
        out_shape=jax.ShapeDtypeStruct((LR_HALO + rows, channels), jnp.bfloat16),
        in_specs=[pl.BlockSpec(memory_space=pltpu.SMEM), vmem]
        + [pl.BlockSpec(memory_space=pl.ANY)] * len(pieces)
        + [vmem] * len(blocks),
        out_specs=vmem,
        scratch_shapes=[
            pltpu.VMEM((rows, depth), jnp.bfloat16),
            pltpu.SemaphoreType.DMA((len(pieces),)),
        ],
        compiler_params=pltpu.CompilerParams(vmem_limit_bytes=44 * MIB),
        cost_estimate=pl.CostEstimate(
            flops=2 * rows * channels * depth, bytes_accessed=4 * rows * depth, transcendentals=0
        ),
        name="stream_rows",
    )(cols, resid, *pieces, *blocks)


def norm_kernel(n_pieces, gain_ref, *refs):
    pieces, out_ref = refs[:n_pieces], refs[n_pieces]
    values = [p[...].astype(jnp.float32) for p in pieces]
    squares = sum(jnp.sum(v * v, axis=1, keepdims=True) for v in values)
    scale = lax.rsqrt(squares / out_ref.shape[1] + norm_eps)
    width = pieces[0].shape[1]
    for i, v in enumerate(values):
        lanes = slice(i * width, (i + 1) * width)
        out_ref[:, lanes] = (v * scale * gain_ref[:, lanes]).astype(jnp.bfloat16)


def norm_rows(gain, pieces):
    rows, width = pieces[0].shape
    depth = width * len(pieces)
    block = 80
    return pl.pallas_call(
        functools.partial(norm_kernel, len(pieces)),
        grid=(rows // block,),
        out_shape=jax.ShapeDtypeStruct((rows, depth), jnp.bfloat16),
        in_specs=[pl.BlockSpec((1, depth), lambda i: (0, 0))]
        + [pl.BlockSpec((block, width), lambda i: (i, 0))] * len(pieces),
        out_specs=pl.BlockSpec((block, depth), lambda i: (i, 0)),
        compiler_params=pltpu.CompilerParams(vmem_limit_bytes=24 * MIB),
        cost_estimate=pl.CostEstimate(
            flops=6 * rows * depth, bytes_accessed=4 * rows * depth, transcendentals=rows
        ),
        name="norm_rows",
    )(gain, *pieces)


def shifted(value, steps):
    place = lax.broadcasted_iota(jnp.int32, value.shape, 0)
    return jnp.where(place >= steps, pltpu.roll(value, steps, 0), 0.0)


def lr_kernel(n_blocks, cols_ref, a_ref, short_ref, rate_ref, residue_ref, *refs):
    blocks = refs[:n_blocks]
    query_ref, local_ref, enter_ref, last_ref, xs, us = refs[n_blocks:]
    rows = a_ref.shape[0] - LR_HALO
    sub = rows // SUBS
    taps = short_ref.shape[1]
    states = rate_ref.shape[0]
    tiles = CHUNK // LANES

    def group(g, _):
        found = project(cols_ref, a_ref, blocks, lambda b: b[g])
        found = found.astype(jnp.bfloat16).astype(jnp.float32)
        for t in range(tiles):
            xs[g * tiles + t] = found[:, t * LANES : (t + 1) * LANES]
        return 0

    lax.fori_loop(0, 3, group, 0)
    for t in range(tiles):
        lanes = slice(t * LANES, (t + 1) * LANES)
        weights = [
            [spread(short_ref[g, pl.ds(j, 1), lanes]) for j in range(taps)] for g in range(3)
        ]

        def features(step, _):
            first = LR_HALO + step * STEP
            queries, keys, values = [
                featurize(xs.at[g * tiles + t], weights[g], first, sub) for g in range(3)
            ]
            for i in range(STEP):
                query_ref[step * STEP + i, :, lanes] = queries[i]
                us[step * STEP + i] = (keys[i] * values[i]).astype(jnp.bfloat16).astype(jnp.float32)
            return 0

        lax.fori_loop(0, sub // STEP, features, 0)
        rate = rate_ref[:, lanes]
        coef = residue_ref[:, lanes] * jnp.sqrt(2.0 * rate)
        decay = jnp.exp(-rate)
        decays = [spread(decay[n : n + 1]) for n in range(states)]
        coefs = [spread(coef[n : n + 1]) for n in range(states)]

        def advance(step, held):
            held = list(held)
            for i in range(4):
                u = us[step * 4 + i]
                terms = []
                for n in range(states):
                    held[n] = decays[n] * held[n] + u
                    terms.append(coefs[n] * held[n])
                while len(terms) > 1:
                    terms = [sum(terms[k : k + 2]) for k in range(0, len(terms), 2)]
                local_ref[step * 4 + i, :, lanes] = terms[0]
            return tuple(held)

        zero = jnp.zeros((SUBS, LANES), jnp.float32)
        held = lax.fori_loop(0, sub // 4, advance, (zero,) * states)
        for n in range(states):
            total = held[n]
            for steps in (1, 2, 4):
                total = total + spread(jnp.exp(-rate[n : n + 1] * (sub * steps))) * shifted(
                    total, steps
                )
            enter_ref[n, :, lanes] = shifted(total, 1)
            last_ref[n : n + 1, lanes] = total[SUBS - 1 : SUBS]


def lr_local(cols, a, short, rate, residue, blocks, first):
    rows = a.shape[0] - LR_HALO
    sub = rows // SUBS
    states = rate.shape[0]
    skip = first // CHUNK
    vmem = pl.BlockSpec(memory_space=pltpu.VMEM)
    depth = a.shape[1]
    return pl.pallas_call(
        functools.partial(lr_kernel, len(blocks)),
        grid=(1,),
        out_shape=(
            jax.ShapeDtypeStruct((sub, SUBS, CHUNK), jnp.float32),
            jax.ShapeDtypeStruct((sub, SUBS, CHUNK), jnp.float32),
            jax.ShapeDtypeStruct((states, SUBS, CHUNK), jnp.float32),
            jax.ShapeDtypeStruct((states, CHUNK), jnp.float32),
        ),
        in_specs=[
            pl.BlockSpec(memory_space=pltpu.SMEM),
            vmem,
            pl.BlockSpec((3, short.shape[1], CHUNK), lambda i: (0, 0, skip)),
            pl.BlockSpec((states, CHUNK), lambda i: (0, skip)),
            pl.BlockSpec((states, CHUNK), lambda i: (0, skip)),
        ]
        + [vmem] * len(blocks),
        out_specs=(vmem, vmem, vmem, vmem),
        scratch_shapes=[
            pltpu.VMEM((3 * (CHUNK // LANES), LR_HALO + rows, LANES), jnp.float32),
            pltpu.VMEM((sub, SUBS, LANES), jnp.float32),
        ],
        compiler_params=pltpu.CompilerParams(vmem_limit_bytes=44 * MIB),
        cost_estimate=pl.CostEstimate(
            flops=2 * rows * 3 * CHUNK * depth, bytes_accessed=4 * rows * depth, transcendentals=0
        ),
        name="lr_local",
    )(cols, a, short, rate, residue, *blocks)


def finish_kernel(n_last, rate_ref, residue_ref, query_ref, local_ref, enter_ref, *refs):
    lasts = refs[:n_last]
    out_ref, of = refs[n_last:]
    sub = query_ref.shape[0]
    rate = rate_ref[...]
    states = rate.shape[0]
    coef = residue_ref[...] * jnp.sqrt(2.0 * rate)
    decay = jnp.exp(-rate)
    device = jnp.exp(-rate * (sub * SUBS))
    incoming = lasts[n_last - 1][...]
    for k in reversed(range(n_last - 1)):
        incoming = incoming * device + lasts[k][...]
    place = lax.broadcasted_iota(jnp.int32, (SUBS, LANES), 0).astype(jnp.float32) * float(sub)
    decays = [spread(decay[n : n + 1]) for n in range(states)]
    held = []
    for n in range(states):
        entering = enter_ref[n] + jnp.exp(-rate[n : n + 1] * place) * incoming[n : n + 1]
        held.append(coef[n : n + 1] * entering)

    def advance(step, held):
        held = list(held)
        for i in range(4):
            r = step * 4 + i
            for n in range(states):
                held[n] = decays[n] * held[n]
            terms = held
            while len(terms) > 1:
                terms = [sum(terms[k : k + 2]) for k in range(0, len(terms), 2)]
            of[pl.ds(r, SUBS, stride=sub), :] = query_ref[r] * (local_ref[r] + terms[0])
        return tuple(held)

    lax.fori_loop(0, sub // 4, advance, tuple(held))
    out_ref[...] = of[...].astype(jnp.bfloat16)


def lr_finish(rate, residue, query, local, enter, lasts, first):
    sub = query.shape[0]
    states = rate.shape[0]
    skip = first // LANES
    return pl.pallas_call(
        functools.partial(finish_kernel, len(lasts)),
        grid=(CHUNK // LANES,),
        out_shape=jax.ShapeDtypeStruct((sub * SUBS, CHUNK), jnp.bfloat16),
        in_specs=[
            pl.BlockSpec((states, LANES), lambda i: (0, i + skip)),
            pl.BlockSpec((states, LANES), lambda i: (0, i + skip)),
            pl.BlockSpec((sub, SUBS, LANES), lambda i: (0, 0, i)),
            pl.BlockSpec((sub, SUBS, LANES), lambda i: (0, 0, i)),
            pl.BlockSpec((states, SUBS, LANES), lambda i: (0, 0, i)),
        ]
        + [pl.BlockSpec((states, LANES), lambda i: (0, i))] * len(lasts),
        out_specs=pl.BlockSpec((sub * SUBS, LANES), lambda i: (0, i)),
        scratch_shapes=[pltpu.VMEM((sub * SUBS, LANES), jnp.float32)],
        compiler_params=pltpu.CompilerParams(vmem_limit_bytes=24 * MIB),
        cost_estimate=pl.CostEstimate(
            flops=sub * SUBS * CHUNK * 40, bytes_accessed=sub * SUBS * CHUNK * 10, transcendentals=0
        ),
        name="lr_finish",
    )(rate, residue, query, local, enter, *lasts)


def after(values, ties):
    if not ties:
        return values
    return lax.optimization_barrier((values, ties))[0]


class Ring:
    def __init__(self, own, order):
        count = len(order)
        self.steps = count // 2
        self.right = [(order[i], order[(i + 1) % count]) for i in range(count)]
        self.left = [(b, a) for a, b in self.right]
        self.ahead, self.behind = [own], [own]

    def step(self, ties):
        k = len(self.ahead)
        a, b = self.ahead[-1], self.behind[-1]
        if k == self.steps:
            half = a.shape[-2] // 2
            a, b = a[..., :half, :], b[..., half:, :]
        a, b = after((a, b), ties)
        self.ahead.append(lax.ppermute(a, "seq", self.right))
        self.behind.append(lax.ppermute(b, "seq", self.left))
        return (self.ahead[-1], self.behind[-1])

    def blocks(self):
        return self.ahead + self.behind[1:]


def block_columns(order, depth, channels):
    count = len(order)
    block = depth // count
    place = lax.axis_index("seq")
    spot = jnp.asarray([order.index(i) for i in range(count)], jnp.int32)[place]
    table = jnp.asarray(order, jnp.int32)
    half = count // 2
    turns = list(range(half + 1)) + [-k for k in range(1, half + 1)]
    source = table[(spot - jnp.asarray(turns, jnp.int32)) % count]
    shift = jnp.asarray([0] * (2 * half) + [block // 2], jnp.int32)
    row = source * block + shift
    peer = jnp.bitwise_xor(row // channels, lax.axis_index("tp"))
    return peer * channels + row % channels


def tp_pieces(own, count):
    def swap(value, mask):
        return lax.ppermute(value, "tp", [(i, i ^ mask) for i in range(count)])

    pieces = [own, swap(own, 1)]
    for mask in range(2, count, 2):
        far = swap(own, mask)
        pieces += [far, swap(far, 1)]
    return pieces


def from_behind(value, steps):
    count = lax.axis_size("seq")
    return lax.ppermute(value, "seq", [(i, i + steps) for i in range(count - steps)])


def per_device(
    mr_qkv,
    residual_in,
    mr_short,
    mr_filter,
    mr_out,
    norm_gain,
    lr_in,
    lr_short,
    lr_rate,
    lr_residue,
):
    rows, _, channels = mr_qkv.shape
    n_seq, n_tp = lax.axis_size("seq"), lax.axis_size("tp")
    depth = channels * n_tp
    order = ring_order(n_seq)
    x = mr_qkv.transpose(1, 0, 2)
    short = mr_short.transpose(1, 0, 2)
    halo = from_behind(x[:, rows - MR_HALO :], 1)
    starts = list(range(0, channels, CHUNK))

    rings = [Ring(mr_out, order)]
    weights = lr_in.transpose(1, 0, 2)
    for first in starts:
        rings.append(Ring(weights[:, :, first : first + CHUNK], order))
    half = rings[0].steps // 2
    plan = [(0, k) for k in range(half)]
    for i in range(len(rings)):
        for k in range(half):
            plan.append((i, half + k))
            if i + 1 < len(rings):
                plan.append((i + 1, k))
    done = []
    for i, _ in plan:
        done.append(rings[i].step(done[-2] if len(done) >= 2 else ()))

    parts = [mr_operator(halo, x, short, mr_filter, first, CHUNK) for first in starts]
    shared = [tp_pieces(part, n_tp) for part in parts]
    pieces = [shared[i][m] for m in range(n_tp) for i in range(len(starts))]
    cols = block_columns(order, depth, channels)
    extended = stream_rows(cols, residual_in, pieces, rings[0].blocks())
    stream = extended[LR_HALO:]
    rim = from_behind(extended[rows:], 1)
    extended = lax.dynamic_update_slice(extended, rim, (0, 0))
    gains = norm_gain.reshape(n_tp, channels)
    peers = jnp.bitwise_xor(jnp.arange(n_tp, dtype=jnp.int32), lax.axis_index("tp"))
    gain = jnp.take(gains, peers, axis=0).reshape(1, depth)
    normed = norm_rows(gain, tp_pieces(extended, n_tp))

    lr_taps = lr_short.transpose(1, 0, 2)
    outs = []
    for i, first in enumerate(starts):
        query, local, enter, last = lr_local(
            cols, normed, lr_taps, lr_rate, lr_residue, rings[i + 1].blocks(), first
        )
        lasts = [from_behind(last, k) for k in range(1, n_seq)]
        outs.append(lr_finish(lr_rate, lr_residue, query, local, enter, lasts, first))
    return (stream, jnp.concatenate(outs, axis=1))


def solution(mesh):
    placed = (
        P("seq", None, "tp"),
        P("seq", "tp"),
        P(None, None, "tp"),
        P(None, "tp"),
        P("seq", "tp"),
        P(),
        P("seq", None, "tp"),
        P(None, None, "tp"),
        P(None, "tp"),
        P(None, "tp"),
    )
    return jax.shard_map(
        per_device,
        mesh=mesh,
        in_specs=placed,
        out_specs=(P("seq", "tp"), P("seq", "tp")),
        check_vma=False,
    )
```

```python
import functools

import jax
import jax.numpy as jnp
from jax import lax
from jax.experimental import pallas as pl
from jax.experimental.pallas import tpu as pltpu
from jax.sharding import PartitionSpec as P

norm_eps = 1e-06
LANES = 128
SUBS = 8
MR_HALO = 144
LR_HALO = 16
CHUNK = 256
STEP = 8
TILE = 16
MIB = 1024 * 1024


def ring_order(count):
    wide = 4 if count % 16 == 0 else 2
    high = count // wide
    order = [z * wide for z in range(high)]
    for turn, z in enumerate(reversed(range(high))):
        cells = range(1, wide) if turn % 2 == 0 else range(wide - 1, 0, -1)
        order += [z * wide + x for x in cells]
    return order


def featurize(ref, weights, first, sub):
    width = len(weights)
    window = [
        ref[pl.ds(first - (width - 1) + i, SUBS, stride=sub), :] for i in range(STEP + width - 1)
    ]
    out = []
    for i in range(STEP):
        total = weights[0] * window[i + width - 1]
        for j in range(1, width):
            total = total + weights[j] * window[i + width - 1 - j]
        out.append(total)
    return out


def lasting(micros):
    return pl.CostEstimate(flops=int(micros * 1.15e9), bytes_accessed=0, transcendentals=0)


def spread(row):
    return jnp.broadcast_to(row, (SUBS, row.shape[-1]))


def mr_kernel(halo_ref, x_ref, short_ref, filter_ref, out_ref, xf, ue, qs, of, ff):
    rows = x_ref.shape[1]
    sub = rows // SUBS
    taps = short_ref.shape[1]
    length = filter_ref.shape[0]
    for g in range(3):
        xf[g, :MR_HALO, :] = halo_ref[g].astype(jnp.float32)
        xf[g, MR_HALO:, :] = x_ref[g].astype(jnp.float32)
    ff[...] = filter_ref[...].astype(jnp.float32)
    weights = [[spread(short_ref[g, pl.ds(j, 1), :]) for j in range(taps)] for g in range(3)]

    def products(step, _):
        first = MR_HALO - sub + step * STEP
        keys = featurize(xf.at[1], weights[1], first, sub)
        values = featurize(xf.at[2], weights[2], first, sub)
        for i in range(STEP):
            ue[step * STEP + i] = (keys[i] * values[i]).astype(jnp.bfloat16).astype(jnp.float32)
        return 0

    lax.fori_loop(0, 2 * sub // STEP, products, 0)

    def queries(step, _):
        found = featurize(xf.at[0], weights[0], MR_HALO + step * STEP, sub)
        for i in range(STEP):
            qs[step * STEP + i] = found[i]
        return 0

    lax.fori_loop(0, sub // STEP, queries, 0)

    def conv(tile, _):
        base = tile * TILE

        def taps_of(part, acc):
            acc = list(acc)
            start = sub + base - part * TILE - (TILE - 1)
            window = [ue[start + m] for m in range(2 * TILE - 1)]
            for j in range(TILE):
                weight = spread(ff[pl.ds(part * TILE + j, 1), :])
                for i in range(TILE):
                    acc[i] = acc[i] + weight * window[i - j + TILE - 1]
            return tuple(acc)

        zero = jnp.zeros((SUBS, LANES), jnp.float32)
        acc = lax.fori_loop(0, length // TILE, taps_of, (zero,) * TILE)
        for i in range(TILE):
            of[pl.ds(base + i, SUBS, stride=sub), :] = acc[i] * qs[base + i]
        return 0

    lax.fori_loop(0, sub // TILE, conv, 0)
    out_ref[...] = of[...].astype(jnp.bfloat16)


def mr_operator(halo, x, short, filters, first, count):
    rows = x.shape[1]
    sub = rows // SUBS
    skip = first // LANES
    return pl.pallas_call(
        mr_kernel,
        grid=(count // LANES,),
        out_shape=jax.ShapeDtypeStruct((rows, count), jnp.bfloat16),
        in_specs=[
            pl.BlockSpec((3, MR_HALO, LANES), lambda i: (0, 0, i + skip)),
            pl.BlockSpec((3, rows, LANES), lambda i: (0, 0, i + skip)),
            pl.BlockSpec((3, short.shape[1], LANES), lambda i: (0, 0, i + skip)),
            pl.BlockSpec((filters.shape[0], LANES), lambda i: (0, i + skip)),
        ],
        out_specs=pl.BlockSpec((rows, LANES), lambda i: (0, i)),
        scratch_shapes=[
            pltpu.VMEM((3, MR_HALO + rows, LANES), jnp.float32),
            pltpu.VMEM((2 * sub, SUBS, LANES), jnp.float32),
            pltpu.VMEM((sub, SUBS, LANES), jnp.float32),
            pltpu.VMEM((rows, LANES), jnp.float32),
            pltpu.VMEM((filters.shape[0], LANES), jnp.float32),
        ],
        compiler_params=pltpu.CompilerParams(vmem_limit_bytes=24 * MIB),
        cost_estimate=lasting(rows * count * 6.8e-5),
        name="mr_operator",
    )(halo, x, short, filters)


def project(cols_ref, a_ref, blocks, pick):
    total = None
    for k, block in enumerate(blocks):
        w = pick(block)
        cols = a_ref[:, pl.ds(pl.multiple_of(cols_ref[k], LANES), w.shape[0])]
        part = jnp.dot(cols, w, preferred_element_type=jnp.float32)
        total = part if total is None else total + part
    return total


def stream_kernel(n_pieces, n_blocks, cols_ref, resid_ref, *refs):
    pieces = refs[:n_pieces]
    blocks = refs[n_pieces : n_pieces + n_blocks]
    out_ref, gated, sems = refs[n_pieces + n_blocks :]
    copies = []
    at = 0
    for i, piece in enumerate(pieces):
        width = piece.shape[1]
        copies.append(pltpu.make_async_copy(piece, gated.at[:, pl.ds(at, width)], sems.at[i]))
        at += width
    for copy in copies:
        copy.start()
    out_ref[:LR_HALO, :] = jnp.zeros((LR_HALO, out_ref.shape[1]), out_ref.dtype)
    for copy in copies:
        copy.wait()

    def tile(i, _):
        lanes = pl.ds(pl.multiple_of(i * CHUNK, CHUNK), CHUNK)
        projected = project(cols_ref, gated, blocks, lambda b: b[:, lanes])
        total = resid_ref[:, lanes].astype(jnp.float32) + projected
        out_ref[LR_HALO:, lanes] = total.astype(jnp.bfloat16)
        return 0

    lax.fori_loop(0, out_ref.shape[1] // CHUNK, tile, 0)


def stream_rows(cols, resid, pieces, blocks):
    rows, channels = resid.shape
    depth = sum(p.shape[1] for p in pieces)
    vmem = pl.BlockSpec(memory_space=pltpu.VMEM)
    return pl.pallas_call(
        functools.partial(stream_kernel, len(pieces), len(blocks)),
        out_shape=jax.ShapeDtypeStruct((LR_HALO + rows, channels), jnp.bfloat16),
        in_specs=[pl.BlockSpec(memory_space=pltpu.SMEM), vmem]
        + [pl.BlockSpec(memory_space=pl.ANY)] * len(pieces)
        + [vmem] * len(blocks),
        out_specs=vmem,
        scratch_shapes=[
            pltpu.VMEM((rows, depth), jnp.bfloat16),
            pltpu.SemaphoreType.DMA((len(pieces),)),
        ],
        compiler_params=pltpu.CompilerParams(vmem_limit_bytes=44 * MIB),
        cost_estimate=lasting(rows * channels * depth * 4e-9),
        name="stream_rows",
    )(cols, resid, *pieces, *blocks)


def norm_kernel(n_pieces, gain_ref, *refs):
    pieces, out_ref = refs[:n_pieces], refs[n_pieces]
    values = [p[...].astype(jnp.float32) for p in pieces]
    squares = sum(jnp.sum(v * v, axis=1, keepdims=True) for v in values)
    scale = lax.rsqrt(squares / out_ref.shape[1] + norm_eps)
    width = pieces[0].shape[1]
    for i, v in enumerate(values):
        lanes = slice(i * width, (i + 1) * width)
        out_ref[:, lanes] = (v * scale * gain_ref[:, lanes]).astype(jnp.bfloat16)


def norm_rows(gain, pieces):
    rows, width = pieces[0].shape
    depth = width * len(pieces)
    block = 80
    return pl.pallas_call(
        functools.partial(norm_kernel, len(pieces)),
        grid=(rows // block,),
        out_shape=jax.ShapeDtypeStruct((rows, depth), jnp.bfloat16),
        in_specs=[pl.BlockSpec((1, depth), lambda i: (0, 0))]
        + [pl.BlockSpec((block, width), lambda i: (i, 0))] * len(pieces),
        out_specs=pl.BlockSpec((block, depth), lambda i: (i, 0)),
        compiler_params=pltpu.CompilerParams(vmem_limit_bytes=24 * MIB),
        cost_estimate=lasting(rows * depth * 2.2e-6),
        name="norm_rows",
    )(gain, *pieces)


def shifted(value, steps):
    place = lax.broadcasted_iota(jnp.int32, value.shape, 0)
    return jnp.where(place >= steps, pltpu.roll(value, steps, 0), 0.0)


def lr_kernel(n_blocks, part, cols_ref, a_ref, short_ref, rate_ref, residue_ref, *refs):
    blocks = refs[:n_blocks]
    query_ref, local_ref, enter_ref, last_ref, xs, us = refs[n_blocks:]
    rows = a_ref.shape[0] - LR_HALO
    sub = rows // SUBS
    taps = short_ref.shape[1]
    states = rate_ref.shape[0]
    tiles = CHUNK // LANES

    def group(g, _):
        found = project(
            cols_ref, a_ref, blocks, lambda b: b[g, :, part * CHUNK : (part + 1) * CHUNK]
        )
        found = found.astype(jnp.bfloat16).astype(jnp.float32)
        for t in range(tiles):
            xs[g * tiles + t] = found[:, t * LANES : (t + 1) * LANES]
        return 0

    lax.fori_loop(0, 3, group, 0)
    for t in range(tiles):
        lanes = slice(t * LANES, (t + 1) * LANES)
        weights = [
            [spread(short_ref[g, pl.ds(j, 1), lanes]) for j in range(taps)] for g in range(3)
        ]

        def features(step, _):
            first = LR_HALO + step * STEP
            queries, keys, values = [
                featurize(xs.at[g * tiles + t], weights[g], first, sub) for g in range(3)
            ]
            for i in range(STEP):
                query_ref[step * STEP + i, :, lanes] = queries[i]
                us[step * STEP + i] = (keys[i] * values[i]).astype(jnp.bfloat16).astype(jnp.float32)
            return 0

        lax.fori_loop(0, sub // STEP, features, 0)
        rate = rate_ref[:, lanes]
        coef = residue_ref[:, lanes] * jnp.sqrt(2.0 * rate)
        decay = jnp.exp(-rate)
        decays = [spread(decay[n : n + 1]) for n in range(states)]
        coefs = [spread(coef[n : n + 1]) for n in range(states)]

        def advance(step, held):
            held = list(held)
            for i in range(4):
                u = us[step * 4 + i]
                terms = []
                for n in range(states):
                    held[n] = decays[n] * held[n] + u
                    terms.append(coefs[n] * held[n])
                while len(terms) > 1:
                    terms = [sum(terms[k : k + 2]) for k in range(0, len(terms), 2)]
                local_ref[step * 4 + i, :, lanes] = terms[0]
            return tuple(held)

        zero = jnp.zeros((SUBS, LANES), jnp.float32)
        held = lax.fori_loop(0, sub // 4, advance, (zero,) * states)
        for n in range(states):
            total = held[n]
            for steps in (1, 2, 4):
                total = total + spread(jnp.exp(-rate[n : n + 1] * (sub * steps))) * shifted(
                    total, steps
                )
            enter_ref[n, :, lanes] = shifted(total, 1)
            last_ref[n : n + 1, lanes] = total[SUBS - 1 : SUBS]


def lr_local(cols, a, short, rate, residue, blocks, first, part):
    rows = a.shape[0] - LR_HALO
    sub = rows // SUBS
    states = rate.shape[0]
    skip = first // CHUNK + part
    vmem = pl.BlockSpec(memory_space=pltpu.VMEM)
    depth = a.shape[1]
    return pl.pallas_call(
        functools.partial(lr_kernel, len(blocks), part),
        grid=(1,),
        out_shape=(
            jax.ShapeDtypeStruct((sub, SUBS, CHUNK), jnp.float32),
            jax.ShapeDtypeStruct((sub, SUBS, CHUNK), jnp.float32),
            jax.ShapeDtypeStruct((states, SUBS, CHUNK), jnp.float32),
            jax.ShapeDtypeStruct((states, CHUNK), jnp.float32),
        ),
        in_specs=[
            pl.BlockSpec(memory_space=pltpu.SMEM),
            vmem,
            pl.BlockSpec((3, short.shape[1], CHUNK), lambda i: (0, 0, skip)),
            pl.BlockSpec((states, CHUNK), lambda i: (0, skip)),
            pl.BlockSpec((states, CHUNK), lambda i: (0, skip)),
        ]
        + [vmem] * len(blocks),
        out_specs=(vmem, vmem, vmem, vmem),
        scratch_shapes=[
            pltpu.VMEM((3 * (CHUNK // LANES), LR_HALO + rows, LANES), jnp.float32),
            pltpu.VMEM((sub, SUBS, LANES), jnp.float32),
        ],
        compiler_params=pltpu.CompilerParams(vmem_limit_bytes=44 * MIB),
        cost_estimate=lasting(rows * CHUNK * depth * 1.7e-8),
        name="lr_local",
    )(cols, a, short, rate, residue, *blocks)


def finish_kernel(n_last, odd_ref, rate_ref, residue_ref, query_ref, local_ref, enter_ref, *refs):
    lasts = refs[:n_last]
    out_ref, of = refs[n_last:]
    sub = query_ref.shape[0]
    rate = rate_ref[...]
    states = rate.shape[0]
    coef = residue_ref[...] * jnp.sqrt(2.0 * rate)
    decay = jnp.exp(-rate)
    device = jnp.exp(-rate * (sub * SUBS))
    incoming = lasts[n_last - 1][...]
    for k in reversed(range(1, n_last - 1)):
        incoming = incoming * (device * device) + lasts[k][...]
    incoming = jnp.where(odd_ref[0] == 1, incoming * device + lasts[0][...], incoming)
    place = lax.broadcasted_iota(jnp.int32, (SUBS, LANES), 0).astype(jnp.float32) * float(sub)
    decays = [spread(decay[n : n + 1]) for n in range(states)]
    held = []
    for n in range(states):
        entering = enter_ref[n] + jnp.exp(-rate[n : n + 1] * place) * incoming[n : n + 1]
        held.append(coef[n : n + 1] * entering)

    def advance(step, held):
        held = list(held)
        for i in range(4):
            r = step * 4 + i
            for n in range(states):
                held[n] = decays[n] * held[n]
            terms = held
            while len(terms) > 1:
                terms = [sum(terms[k : k + 2]) for k in range(0, len(terms), 2)]
            of[pl.ds(r, SUBS, stride=sub), :] = query_ref[r] * (local_ref[r] + terms[0])
        return tuple(held)

    lax.fori_loop(0, sub // 4, advance, tuple(held))
    out_ref[...] = of[...].astype(jnp.bfloat16)


def lr_finish(odd, rate, residue, query, local, enter, lasts, first, part):
    sub = query.shape[0]
    states = rate.shape[0]
    past = part * (CHUNK // LANES)
    skip = first // LANES + past
    return pl.pallas_call(
        functools.partial(finish_kernel, len(lasts)),
        grid=(CHUNK // LANES,),
        out_shape=jax.ShapeDtypeStruct((sub * SUBS, CHUNK), jnp.bfloat16),
        in_specs=[
            pl.BlockSpec(memory_space=pltpu.SMEM),
            pl.BlockSpec((states, LANES), lambda i: (0, i + skip)),
            pl.BlockSpec((states, LANES), lambda i: (0, i + skip)),
            pl.BlockSpec((sub, SUBS, LANES), lambda i: (0, 0, i)),
            pl.BlockSpec((sub, SUBS, LANES), lambda i: (0, 0, i)),
            pl.BlockSpec((states, SUBS, LANES), lambda i: (0, 0, i)),
        ]
        + [pl.BlockSpec((states, LANES), lambda i: (0, i + past))] * len(lasts),
        out_specs=pl.BlockSpec((sub * SUBS, LANES), lambda i: (0, i)),
        scratch_shapes=[pltpu.VMEM((sub * SUBS, LANES), jnp.float32)],
        compiler_params=pltpu.CompilerParams(vmem_limit_bytes=24 * MIB),
        cost_estimate=lasting(sub * SUBS * CHUNK * 8e-6),
        name="lr_finish",
    )(odd, rate, residue, query, local, enter, *lasts)


def after(values, ties):
    if not ties:
        return values
    return lax.optimization_barrier((values, ties))[0]


class Ring:
    def __init__(self, own, order):
        count = len(order)
        self.steps = count // 2
        self.right = [(order[i], order[(i + 1) % count]) for i in range(count)]
        self.left = [(b, a) for a, b in self.right]
        self.ahead, self.behind = [own], [own]

    def step(self, ties):
        k = len(self.ahead)
        a, b = self.ahead[-1], self.behind[-1]
        if k == self.steps:
            half = a.shape[-2] // 2
            a, b = a[..., :half, :], b[..., half:, :]
        a, b = after((a, b), ties)
        self.ahead.append(lax.ppermute(a, "seq", self.right))
        self.behind.append(lax.ppermute(b, "seq", self.left))
        return (self.ahead[-1], self.behind[-1])

    def blocks(self):
        return self.ahead + self.behind[1:]


def block_columns(order, depth, channels):
    count = len(order)
    block = depth // count
    place = lax.axis_index("seq")
    spot = jnp.asarray([order.index(i) for i in range(count)], jnp.int32)[place]
    table = jnp.asarray(order, jnp.int32)
    half = count // 2
    turns = list(range(half + 1)) + [-k for k in range(1, half + 1)]
    source = table[(spot - jnp.asarray(turns, jnp.int32)) % count]
    shift = jnp.asarray([0] * (2 * half) + [block // 2], jnp.int32)
    row = source * block + shift
    peer = jnp.bitwise_xor(row // channels, lax.axis_index("tp"))
    return peer * channels + row % channels


def swap_tp(value, mask):
    count = lax.axis_size("tp")
    return lax.ppermute(value, "tp", [(i, i ^ mask) for i in range(count)])


def tp_pieces(own, count, ties):
    pieces = [own, swap_tp(own, 1)]
    for mask in range(2, count, 2):
        far = swap_tp(own, mask)
        pieces += [far, swap_tp(after(far, ties), 1)]
    return pieces


def from_behind(value, steps):
    count = lax.axis_size("seq")
    return lax.ppermute(value, "seq", [(i, i + steps) for i in range(count - steps)])


def earlier_states(last, rate, rows):
    count = lax.axis_size("seq")
    odd = lax.rem(lax.axis_index("seq"), 2)
    other = lax.ppermute(last, "seq", [(i, i ^ 1) for i in range(count)])
    first, second = jnp.where(odd == 1, other, last), jnp.where(odd == 1, last, other)
    both = first * jnp.exp(-rate * rows) + second
    return odd.reshape(1), other, [from_behind(both, 2 * k) for k in range(1, count // 2)]


def per_device(
    mr_qkv,
    residual_in,
    mr_short,
    mr_filter,
    mr_out,
    norm_gain,
    lr_in,
    lr_short,
    lr_rate,
    lr_residue,
):
    rows, _, channels = mr_qkv.shape
    n_seq, n_tp = lax.axis_size("seq"), lax.axis_size("tp")
    depth = channels * n_tp
    order = ring_order(n_seq)
    x = mr_qkv.transpose(1, 0, 2)
    short = mr_short.transpose(1, 0, 2)
    halo = from_behind(x[:, rows - MR_HALO :], 1)
    starts = list(range(0, channels, CHUNK))
    final = len(starts)
    wide = [2 * CHUNK] * (channels >= 4 * CHUNK)
    wide += [CHUNK] * ((channels - sum(wide)) // CHUNK)

    rings = [Ring(mr_out, order)]
    weights = lr_in.transpose(1, 0, 2)
    first = 0
    for width in wide:
        rings.append(Ring(weights[:, :, first : first + width], order))
        first += width
    steps = rings[0].steps
    begins = [0] + [steps - 1 + i * (steps - 2) for i in range(len(wide))]
    plan = [
        [(i, turn - begin) for i, begin in enumerate(begins) if 0 <= turn - begin < steps]
        for turn in range(begins[-1] + steps)
    ]
    turns = len(plan)
    waits = {}
    done = []

    def drive(turn):
        while len(done) < min(turn, turns):
            now = len(done)
            ties = tuple(waits.get(now, ()))
            got = []
            for i, k in plan[now]:
                fresh = k == 0 and now > 0
                got += rings[i].step(ties + (tuple(done[-1][:2]) if fresh else ()))
            done.append(got)
        return tuple(done[min(turn, turns) - 1]) if turn > 0 else ()

    def hold(turn, value):
        waits.setdefault(turn + 1, []).append(value)

    waits[0] = [halo]
    parts, near, far, passed = [], [], [], []
    for i, first in enumerate(starts):
        ties = drive(i)
        if i >= 2:
            ties += tuple(far[i - 2])
        if i >= 3:
            ties += tuple(passed[i - 3])
        parts.append(mr_operator(halo, x, after(short, ties), mr_filter, first, CHUNK))
        hold(i, parts[-1])
        if i > 0:
            passed.append([swap_tp(after(f, [parts[i]]), 1) for f in far[i - 1]])
        part = parts[-1] if i < final - 1 else after(parts[-1], drive(steps)[:2])
        near.append(swap_tp(parts[-1], 1))
        far.append([swap_tp(part, mask) for mask in range(2, n_tp, 2)])
    passed.append([swap_tp(f, 1) for f in far[-1]])
    pieces = []
    for m in range(n_tp):
        for i in range(final):
            if m < 2:
                pieces.append((parts, near)[m][i])
            else:
                pieces.append((far, passed)[m % 2][i][m // 2 - 1])
    cols = after(block_columns(order, depth, channels), drive(steps))
    extended = stream_rows(cols, residual_in, pieces, rings[0].blocks())
    stream = extended[LR_HALO:]
    rim = from_behind(extended[rows:], 1)
    extended = lax.dynamic_update_slice(extended, rim, (0, 0))
    gains = norm_gain.reshape(n_tp, channels)
    peers = jnp.bitwise_xor(jnp.arange(n_tp, dtype=jnp.int32), lax.axis_index("tp"))
    gain = jnp.take(gains, peers, axis=0).reshape(1, depth)
    shared = tp_pieces(extended, n_tp, drive(steps + 1))
    turn = steps + 2
    normed = norm_rows(after(gain, drive(turn)), shared)
    hold(turn, normed)

    lr_taps = lr_short.transpose(1, 0, 2)
    found = []
    first = 0
    for i, width in enumerate(wide):
        turn = begins[i + 1] + steps - 1
        drive(turn + 1)
        taps = lr_taps
        for part in range(width // CHUNK):
            if part > 0:
                taps = after(lr_taps, drive(turn + 1))
            found.append(
                lr_local(cols, normed, taps, lr_rate, lr_residue, rings[i + 1].blocks(), first, part)
            )
            hold(turn + 1, found[-1][3])
        first += width
    odd, other, fars = earlier_states(
        jnp.concatenate([f[3] for f in found], axis=1), lr_rate, rows
    )
    outs = [
        lr_finish(odd, lr_rate, lr_residue, query, local, enter, [other] + fars, 0, part)
        for part, (query, local, enter, _) in enumerate(found)
    ]
    return (stream, jnp.concatenate(outs, axis=1))


def solution(mesh):
    placed = (
        P("seq", None, "tp"),
        P("seq", "tp"),
        P(None, None, "tp"),
        P(None, "tp"),
        P("seq", "tp"),
        P(),
        P("seq", None, "tp"),
        P(None, None, "tp"),
        P(None, "tp"),
        P(None, "tp"),
    )
    return jax.shard_map(
        per_device,
        mesh=mesh,
        in_specs=placed,
        out_specs=(P("seq", "tp"), P("seq", "tp")),
        check_vma=False,
    )
```

```python
import functools

import jax
import jax.numpy as jnp
from jax import lax
from jax.experimental import pallas as pl
from jax.experimental.pallas import tpu as pltpu
from jax.sharding import PartitionSpec as P

norm_eps = 1e-06
LANES = 128
SUBS = 8
MR_HALO = 144
LR_HALO = 16
CHUNK = 256
STEP = 8
TILE = 16
MIB = 1024 * 1024


def ring_order(count):
    wide = 4 if count % 16 == 0 else 2
    high = count // wide
    order = [z * wide for z in range(high)]
    for turn, z in enumerate(reversed(range(high))):
        cells = range(1, wide) if turn % 2 == 0 else range(wide - 1, 0, -1)
        order += [z * wide + x for x in cells]
    return order


def featurize(ref, weights, first, sub):
    width = len(weights)
    window = [
        ref[pl.ds(first - (width - 1) + i, SUBS, stride=sub), :] for i in range(STEP + width - 1)
    ]
    out = []
    for i in range(STEP):
        total = weights[0] * window[i + width - 1]
        for j in range(1, width):
            total = total + weights[j] * window[i + width - 1 - j]
        out.append(total)
    return out


def lasting(micros):
    return pl.CostEstimate(flops=int(micros * 1.15e9), bytes_accessed=0, transcendentals=0)


def spread(row):
    return jnp.broadcast_to(row, (SUBS, row.shape[-1]))


def mr_kernel(halo_ref, x_ref, short_ref, filter_ref, out_ref, xf, ue, qs, of, ff):
    rows = x_ref.shape[1]
    sub = rows // SUBS
    taps = short_ref.shape[1]
    length = filter_ref.shape[0]
    for g in range(3):
        xf[g, :MR_HALO, :] = halo_ref[g].astype(jnp.float32)
        xf[g, MR_HALO:, :] = x_ref[g].astype(jnp.float32)
    ff[...] = filter_ref[...].astype(jnp.float32)
    weights = [[spread(short_ref[g, pl.ds(j, 1), :]) for j in range(taps)] for g in range(3)]

    def products(step, _):
        first = MR_HALO - sub + step * STEP
        keys = featurize(xf.at[1], weights[1], first, sub)
        values = featurize(xf.at[2], weights[2], first, sub)
        for i in range(STEP):
            ue[step * STEP + i] = (keys[i] * values[i]).astype(jnp.bfloat16).astype(jnp.float32)
        return 0

    lax.fori_loop(0, 2 * sub // STEP, products, 0)

    def queries(step, _):
        found = featurize(xf.at[0], weights[0], MR_HALO + step * STEP, sub)
        for i in range(STEP):
            qs[step * STEP + i] = found[i]
        return 0

    lax.fori_loop(0, sub // STEP, queries, 0)

    def conv(tile, _):
        base = tile * TILE

        def taps_of(part, acc):
            acc = list(acc)
            start = sub + base - part * TILE - (TILE - 1)
            window = [ue[start + m] for m in range(2 * TILE - 1)]
            for j in range(TILE):
                weight = spread(ff[pl.ds(part * TILE + j, 1), :])
                for i in range(TILE):
                    acc[i] = acc[i] + weight * window[i - j + TILE - 1]
            return tuple(acc)

        zero = jnp.zeros((SUBS, LANES), jnp.float32)
        acc = lax.fori_loop(0, length // TILE, taps_of, (zero,) * TILE)
        for i in range(TILE):
            of[pl.ds(base + i, SUBS, stride=sub), :] = acc[i] * qs[base + i]
        return 0

    lax.fori_loop(0, sub // TILE, conv, 0)
    out_ref[...] = of[...].astype(jnp.bfloat16)


def mr_operator(halo, x, short, filters, first, count):
    rows = x.shape[1]
    sub = rows // SUBS
    skip = first // LANES
    return pl.pallas_call(
        mr_kernel,
        grid=(count // LANES,),
        out_shape=jax.ShapeDtypeStruct((rows, count), jnp.bfloat16),
        in_specs=[
            pl.BlockSpec((3, MR_HALO, LANES), lambda i: (0, 0, i + skip)),
            pl.BlockSpec((3, rows, LANES), lambda i: (0, 0, i + skip)),
            pl.BlockSpec((3, short.shape[1], LANES), lambda i: (0, 0, i + skip)),
            pl.BlockSpec((filters.shape[0], LANES), lambda i: (0, i + skip)),
        ],
        out_specs=pl.BlockSpec((rows, LANES), lambda i: (0, i)),
        scratch_shapes=[
            pltpu.VMEM((3, MR_HALO + rows, LANES), jnp.float32),
            pltpu.VMEM((2 * sub, SUBS, LANES), jnp.float32),
            pltpu.VMEM((sub, SUBS, LANES), jnp.float32),
            pltpu.VMEM((rows, LANES), jnp.float32),
            pltpu.VMEM((filters.shape[0], LANES), jnp.float32),
        ],
        compiler_params=pltpu.CompilerParams(vmem_limit_bytes=24 * MIB),
        cost_estimate=lasting(rows * count * 6.8e-5),
        name="mr_operator",
    )(halo, x, short, filters)


def project(cols_ref, a_ref, blocks, pick):
    total = None
    for k, block in enumerate(blocks):
        w = pick(block)
        cols = a_ref[:, pl.ds(pl.multiple_of(cols_ref[k], LANES), w.shape[0])]
        part = jnp.dot(cols, w, preferred_element_type=jnp.float32)
        total = part if total is None else total + part
    return total


def stream_kernel(n_pieces, n_blocks, cols_ref, resid_ref, *refs):
    pieces = refs[:n_pieces]
    blocks = refs[n_pieces : n_pieces + n_blocks]
    out_ref, gated, sems = refs[n_pieces + n_blocks :]
    copies = []
    at = 0
    for i, piece in enumerate(pieces):
        width = piece.shape[1]
        copies.append(pltpu.make_async_copy(piece, gated.at[:, pl.ds(at, width)], sems.at[i]))
        at += width
    for copy in copies:
        copy.start()
    out_ref[:LR_HALO, :] = jnp.zeros((LR_HALO, out_ref.shape[1]), out_ref.dtype)
    for copy in copies:
        copy.wait()

    def tile(i, _):
        lanes = pl.ds(pl.multiple_of(i * CHUNK, CHUNK), CHUNK)
        projected = project(cols_ref, gated, blocks, lambda b: b[:, lanes])
        total = resid_ref[:, lanes].astype(jnp.float32) + projected
        out_ref[LR_HALO:, lanes] = total.astype(jnp.bfloat16)
        return 0

    lax.fori_loop(0, out_ref.shape[1] // CHUNK, tile, 0)


def stream_rows(cols, resid, pieces, blocks):
    rows, channels = resid.shape
    depth = sum(p.shape[1] for p in pieces)
    vmem = pl.BlockSpec(memory_space=pltpu.VMEM)
    return pl.pallas_call(
        functools.partial(stream_kernel, len(pieces), len(blocks)),
        out_shape=jax.ShapeDtypeStruct((LR_HALO + rows, channels), jnp.bfloat16),
        in_specs=[pl.BlockSpec(memory_space=pltpu.SMEM), vmem]
        + [pl.BlockSpec(memory_space=pl.ANY)] * len(pieces)
        + [vmem] * len(blocks),
        out_specs=vmem,
        scratch_shapes=[
            pltpu.VMEM((rows, depth), jnp.bfloat16),
            pltpu.SemaphoreType.DMA((len(pieces),)),
        ],
        compiler_params=pltpu.CompilerParams(vmem_limit_bytes=44 * MIB),
        cost_estimate=lasting(rows * channels * depth * 4e-9),
        name="stream_rows",
    )(cols, resid, *pieces, *blocks)


def norm_kernel(n_pieces, gain_ref, *refs):
    pieces, out_ref = refs[:n_pieces], refs[n_pieces]
    values = [p[...].astype(jnp.float32) for p in pieces]
    squares = sum(jnp.sum(v * v, axis=1, keepdims=True) for v in values)
    scale = lax.rsqrt(squares / out_ref.shape[1] + norm_eps)
    width = pieces[0].shape[1]
    for i, v in enumerate(values):
        lanes = slice(i * width, (i + 1) * width)
        out_ref[:, lanes] = (v * scale * gain_ref[:, lanes]).astype(jnp.bfloat16)


def norm_rows(gain, pieces):
    rows, width = pieces[0].shape
    depth = width * len(pieces)
    block = 80
    return pl.pallas_call(
        functools.partial(norm_kernel, len(pieces)),
        grid=(rows // block,),
        out_shape=jax.ShapeDtypeStruct((rows, depth), jnp.bfloat16),
        in_specs=[pl.BlockSpec((1, depth), lambda i: (0, 0))]
        + [pl.BlockSpec((block, width), lambda i: (i, 0))] * len(pieces),
        out_specs=pl.BlockSpec((block, depth), lambda i: (i, 0)),
        compiler_params=pltpu.CompilerParams(vmem_limit_bytes=24 * MIB),
        cost_estimate=lasting(rows * depth * 2.2e-6),
        name="norm_rows",
    )(gain, *pieces)


def shifted(value, steps):
    place = lax.broadcasted_iota(jnp.int32, value.shape, 0)
    return jnp.where(place >= steps, pltpu.roll(value, steps, 0), 0.0)


def lr_kernel(n_blocks, part, cols_ref, a_ref, short_ref, rate_ref, residue_ref, *refs):
    blocks = refs[:n_blocks]
    query_ref, local_ref, enter_ref, last_ref, xs, us = refs[n_blocks:]
    rows = a_ref.shape[0] - LR_HALO
    sub = rows // SUBS
    taps = short_ref.shape[1]
    states = rate_ref.shape[0]
    tiles = CHUNK // LANES

    def group(g, _):
        found = project(
            cols_ref, a_ref, blocks, lambda b: b[g, :, part * CHUNK : (part + 1) * CHUNK]
        )
        found = found.astype(jnp.bfloat16).astype(jnp.float32)
        for t in range(tiles):
            xs[g * tiles + t] = found[:, t * LANES : (t + 1) * LANES]
        return 0

    lax.fori_loop(0, 3, group, 0)
    for t in range(tiles):
        lanes = slice(t * LANES, (t + 1) * LANES)
        weights = [
            [spread(short_ref[g, pl.ds(j, 1), lanes]) for j in range(taps)] for g in range(3)
        ]

        def features(step, _):
            first = LR_HALO + step * STEP
            queries, keys, values = [
                featurize(xs.at[g * tiles + t], weights[g], first, sub) for g in range(3)
            ]
            for i in range(STEP):
                query_ref[step * STEP + i, :, lanes] = queries[i]
                us[step * STEP + i] = (keys[i] * values[i]).astype(jnp.bfloat16).astype(jnp.float32)
            return 0

        lax.fori_loop(0, sub // STEP, features, 0)
        rate = rate_ref[:, lanes]
        coef = residue_ref[:, lanes] * jnp.sqrt(2.0 * rate)
        decay = jnp.exp(-rate)
        decays = [spread(decay[n : n + 1]) for n in range(states)]
        coefs = [spread(coef[n : n + 1]) for n in range(states)]

        def advance(step, held):
            held = list(held)
            for i in range(4):
                u = us[step * 4 + i]
                terms = []
                for n in range(states):
                    held[n] = decays[n] * held[n] + u
                    terms.append(coefs[n] * held[n])
                while len(terms) > 1:
                    terms = [sum(terms[k : k + 2]) for k in range(0, len(terms), 2)]
                local_ref[step * 4 + i, :, lanes] = terms[0]
            return tuple(held)

        zero = jnp.zeros((SUBS, LANES), jnp.float32)
        held = lax.fori_loop(0, sub // 4, advance, (zero,) * states)
        for n in range(states):
            total = held[n]
            for steps in (1, 2, 4):
                total = total + spread(jnp.exp(-rate[n : n + 1] * (sub * steps))) * shifted(
                    total, steps
                )
            enter_ref[n, :, lanes] = shifted(total, 1)
            last_ref[n : n + 1, lanes] = total[SUBS - 1 : SUBS]


def lr_local(cols, a, short, rate, residue, blocks, first, part):
    rows = a.shape[0] - LR_HALO
    sub = rows // SUBS
    states = rate.shape[0]
    skip = first // CHUNK + part
    vmem = pl.BlockSpec(memory_space=pltpu.VMEM)
    depth = a.shape[1]
    return pl.pallas_call(
        functools.partial(lr_kernel, len(blocks), part),
        grid=(1,),
        out_shape=(
            jax.ShapeDtypeStruct((sub, SUBS, CHUNK), jnp.float32),
            jax.ShapeDtypeStruct((sub, SUBS, CHUNK), jnp.float32),
            jax.ShapeDtypeStruct((states, SUBS, CHUNK), jnp.float32),
            jax.ShapeDtypeStruct((states, CHUNK), jnp.float32),
        ),
        in_specs=[
            pl.BlockSpec(memory_space=pltpu.SMEM),
            vmem,
            pl.BlockSpec((3, short.shape[1], CHUNK), lambda i: (0, 0, skip)),
            pl.BlockSpec((states, CHUNK), lambda i: (0, skip)),
            pl.BlockSpec((states, CHUNK), lambda i: (0, skip)),
        ]
        + [vmem] * len(blocks),
        out_specs=(vmem, vmem, vmem, vmem),
        scratch_shapes=[
            pltpu.VMEM((3 * (CHUNK // LANES), LR_HALO + rows, LANES), jnp.float32),
            pltpu.VMEM((sub, SUBS, LANES), jnp.float32),
        ],
        compiler_params=pltpu.CompilerParams(vmem_limit_bytes=44 * MIB),
        cost_estimate=lasting(rows * CHUNK * depth * 1.7e-8),
        name="lr_local",
    )(cols, a, short, rate, residue, *blocks)


def finish_kernel(n_last, odd_ref, rate_ref, residue_ref, query_ref, local_ref, enter_ref, *refs):
    lasts = refs[:n_last]
    out_ref, of = refs[n_last:]
    sub = query_ref.shape[0]
    rate = rate_ref[...]
    states = rate.shape[0]
    coef = residue_ref[...] * jnp.sqrt(2.0 * rate)
    decay = jnp.exp(-rate)
    device = jnp.exp(-rate * (sub * SUBS))
    incoming = lasts[n_last - 1][...]
    for k in reversed(range(1, n_last - 1)):
        incoming = incoming * (device * device) + lasts[k][...]
    incoming = jnp.where(odd_ref[0] == 1, incoming * device + lasts[0][...], incoming)
    place = lax.broadcasted_iota(jnp.int32, (SUBS, LANES), 0).astype(jnp.float32) * float(sub)
    decays = [spread(decay[n : n + 1]) for n in range(states)]
    held = []
    for n in range(states):
        entering = enter_ref[n] + jnp.exp(-rate[n : n + 1] * place) * incoming[n : n + 1]
        held.append(coef[n : n + 1] * entering)

    def advance(step, held):
        held = list(held)
        for i in range(4):
            r = step * 4 + i
            for n in range(states):
                held[n] = decays[n] * held[n]
            terms = held
            while len(terms) > 1:
                terms = [sum(terms[k : k + 2]) for k in range(0, len(terms), 2)]
            of[pl.ds(r, SUBS, stride=sub), :] = query_ref[r] * (local_ref[r] + terms[0])
        return tuple(held)

    lax.fori_loop(0, sub // 4, advance, tuple(held))
    out_ref[...] = of[...].astype(jnp.bfloat16)


def lr_finish(odd, rate, residue, query, local, enter, lasts, first, part):
    sub = query.shape[0]
    states = rate.shape[0]
    past = part * (CHUNK // LANES)
    skip = first // LANES + past
    return pl.pallas_call(
        functools.partial(finish_kernel, len(lasts)),
        grid=(CHUNK // LANES,),
        out_shape=jax.ShapeDtypeStruct((sub * SUBS, CHUNK), jnp.bfloat16),
        in_specs=[
            pl.BlockSpec(memory_space=pltpu.SMEM),
            pl.BlockSpec((states, LANES), lambda i: (0, i + skip)),
            pl.BlockSpec((states, LANES), lambda i: (0, i + skip)),
            pl.BlockSpec((sub, SUBS, LANES), lambda i: (0, 0, i)),
            pl.BlockSpec((sub, SUBS, LANES), lambda i: (0, 0, i)),
            pl.BlockSpec((states, SUBS, LANES), lambda i: (0, 0, i)),
        ]
        + [pl.BlockSpec((states, LANES), lambda i: (0, i + past))] * len(lasts),
        out_specs=pl.BlockSpec((sub * SUBS, LANES), lambda i: (0, i)),
        scratch_shapes=[pltpu.VMEM((sub * SUBS, LANES), jnp.float32)],
        compiler_params=pltpu.CompilerParams(vmem_limit_bytes=24 * MIB),
        cost_estimate=lasting(sub * SUBS * CHUNK * 8e-6),
        name="lr_finish",
    )(odd, rate, residue, query, local, enter, *lasts)


def after(values, ties):
    if not ties:
        return values
    return lax.optimization_barrier((values, ties))[0]


class Ring:
    def __init__(self, own, order):
        count = len(order)
        self.steps = count // 2
        self.right = [(order[i], order[(i + 1) % count]) for i in range(count)]
        self.left = [(b, a) for a, b in self.right]
        self.ahead, self.behind = [own], [own]

    def step(self, ties):
        k = len(self.ahead)
        a, b = self.ahead[-1], self.behind[-1]
        if k == self.steps:
            half = a.shape[-2] // 2
            a, b = a[..., :half, :], b[..., half:, :]
        a, b = after((a, b), ties)
        self.ahead.append(lax.ppermute(a, "seq", self.right))
        self.behind.append(lax.ppermute(b, "seq", self.left))
        return (self.ahead[-1], self.behind[-1])

    def blocks(self):
        return self.ahead + self.behind[1:]


def block_columns(order, depth, channels):
    count = len(order)
    block = depth // count
    place = lax.axis_index("seq")
    spot = jnp.asarray([order.index(i) for i in range(count)], jnp.int32)[place]
    table = jnp.asarray(order, jnp.int32)
    half = count // 2
    turns = list(range(half + 1)) + [-k for k in range(1, half + 1)]
    source = table[(spot - jnp.asarray(turns, jnp.int32)) % count]
    shift = jnp.asarray([0] * (2 * half) + [block // 2], jnp.int32)
    row = source * block + shift
    peer = jnp.bitwise_xor(row // channels, lax.axis_index("tp"))
    return peer * channels + row % channels


def swap_tp(value, mask):
    count = lax.axis_size("tp")
    return lax.ppermute(value, "tp", [(i, i ^ mask) for i in range(count)])


def tp_pieces(own, count, ties):
    pieces = [own, swap_tp(own, 1)]
    for mask in range(2, count, 2):
        far = swap_tp(own, mask)
        pieces += [far, swap_tp(after(far, ties), 1)]
    return pieces


def from_behind(value, steps):
    count = lax.axis_size("seq")
    return lax.ppermute(value, "seq", [(i, i + steps) for i in range(count - steps)])


def earlier_states(last, rate, rows):
    count = lax.axis_size("seq")
    odd = lax.rem(lax.axis_index("seq"), 2)
    other = lax.ppermute(last, "seq", [(i, i ^ 1) for i in range(count)])
    first, second = jnp.where(odd == 1, other, last), jnp.where(odd == 1, last, other)
    both = first * jnp.exp(-rate * rows) + second
    return odd.reshape(1), other, [from_behind(both, 2 * k) for k in range(1, count // 2)]


def per_device(
    mr_qkv,
    residual_in,
    mr_short,
    mr_filter,
    mr_out,
    norm_gain,
    lr_in,
    lr_short,
    lr_rate,
    lr_residue,
):
    rows, _, channels = mr_qkv.shape
    n_seq, n_tp = lax.axis_size("seq"), lax.axis_size("tp")
    depth = channels * n_tp
    order = ring_order(n_seq)
    x = mr_qkv.transpose(1, 0, 2)
    short = mr_short.transpose(1, 0, 2)
    halo = from_behind(x[:, rows - MR_HALO :], 1)
    starts = list(range(0, channels, CHUNK))
    final = len(starts)
    wide = [2 * CHUNK] * (channels >= 4 * CHUNK)
    wide += [CHUNK] * ((channels - sum(wide)) // CHUNK)

    rings = [Ring(mr_out, order)]
    weights = lr_in.transpose(1, 0, 2)
    first = 0
    for width in wide:
        rings.append(Ring(weights[:, :, first : first + width], order))
        first += width
    steps = rings[0].steps
    begins = [0] + [steps - 1 + i * (steps - 2) for i in range(len(wide))]
    plan = [
        [(i, turn - begin) for i, begin in enumerate(begins) if 0 <= turn - begin < steps]
        for turn in range(begins[-1] + steps)
    ]
    turns = len(plan)
    waits = {}
    done = []

    def drive(turn):
        while len(done) < min(turn, turns):
            now = len(done)
            ties = tuple(waits.get(now, ()))
            got = []
            for i, k in plan[now]:
                fresh = k == 0 and now > 0
                got += rings[i].step(ties + (tuple(done[-1][:2]) if fresh else ()))
            done.append(got)
        return tuple(done[min(turn, turns) - 1]) if turn > 0 else ()

    def hold(turn, value):
        waits.setdefault(turn + 1, []).append(value)

    waits[0] = [halo]
    parts, near, far, passed = [], [], [], []
    for i, first in enumerate(starts):
        ties = drive(i)
        if i >= 2:
            ties += tuple(far[i - 2])
        if i >= 3:
            ties += tuple(passed[i - 3])
        parts.append(mr_operator(halo, x, after(short, ties), mr_filter, first, CHUNK))
        hold(i, parts[-1])
        if i > 0:
            passed.append([swap_tp(after(f, [parts[i]]), 1) for f in far[i - 1]])
        part = parts[-1] if i < final - 1 else after(parts[-1], drive(steps)[:2])
        near.append(swap_tp(parts[-1], 1))
        far.append([swap_tp(part, mask) for mask in range(2, n_tp, 2)])
    passed.append([swap_tp(f, 1) for f in far[-1]])
    pieces = []
    for m in range(n_tp):
        for i in range(final):
            if m < 2:
                pieces.append((parts, near)[m][i])
            else:
                pieces.append((far, passed)[m % 2][i][m // 2 - 1])
    cols = after(block_columns(order, depth, channels), drive(steps))
    extended = stream_rows(cols, residual_in, pieces, rings[0].blocks())
    stream = extended[LR_HALO:]
    rim = from_behind(extended[rows:], 1)
    extended = lax.dynamic_update_slice(extended, rim, (0, 0))
    gains = norm_gain.reshape(n_tp, channels)
    peers = jnp.bitwise_xor(jnp.arange(n_tp, dtype=jnp.int32), lax.axis_index("tp"))
    gain = jnp.take(gains, peers, axis=0).reshape(1, depth)
    shared = tp_pieces(extended, n_tp, drive(steps + 1))
    turn = steps + 2
    normed = norm_rows(after(gain, drive(turn)), shared)

    lr_taps = lr_short.transpose(1, 0, 2)
    found = []
    first = 0
    for i, width in enumerate(wide):
        turn = begins[i + 1] + steps - 1
        drive(turn + 1)
        taps = lr_taps
        for part in range(width // CHUNK):
            if part > 0:
                taps = after(lr_taps, drive(turn + 2))
            found.append(
                lr_local(cols, normed, taps, lr_rate, lr_residue, rings[i + 1].blocks(), first, part)
            )
            hold(turn + 1 + part, found[-1][3])
        first += width
    odd, other, fars = earlier_states(
        jnp.concatenate([f[3] for f in found], axis=1), lr_rate, rows
    )
    outs = [
        lr_finish(odd, lr_rate, lr_residue, query, local, enter, [other] + fars, 0, part)
        for part, (query, local, enter, _) in enumerate(found)
    ]
    return (stream, jnp.concatenate(outs, axis=1))


def solution(mesh):
    placed = (
        P("seq", None, "tp"),
        P("seq", "tp"),
        P(None, None, "tp"),
        P(None, "tp"),
        P("seq", "tp"),
        P(),
        P("seq", None, "tp"),
        P(None, None, "tp"),
        P(None, "tp"),
        P(None, "tp"),
    )
    return jax.shard_map(
        per_device,
        mesh=mesh,
        in_specs=placed,
        out_specs=(P("seq", "tp"), P("seq", "tp")),
        check_vma=False,
    )
```

```python
import functools

import jax
import jax.numpy as jnp
from jax import lax
from jax.experimental import pallas as pl
from jax.experimental.pallas import tpu as pltpu
from jax.sharding import PartitionSpec as P

norm_eps = 1e-06
LANES = 128
SUBS = 8
MR_HALO = 144
LR_HALO = 16
CHUNK = 256
STEP = 8
TILE = 16
MIB = 1024 * 1024


def ring_order(count):
    wide = 4 if count % 16 == 0 else 2
    high = count // wide
    order = [z * wide for z in range(high)]
    for turn, z in enumerate(reversed(range(high))):
        cells = range(1, wide) if turn % 2 == 0 else range(wide - 1, 0, -1)
        order += [z * wide + x for x in cells]
    return order


def featurize(ref, weights, first, sub):
    width = len(weights)
    window = [
        ref[pl.ds(first - (width - 1) + i, SUBS, stride=sub), :] for i in range(STEP + width - 1)
    ]
    out = []
    for i in range(STEP):
        total = weights[0] * window[i + width - 1]
        for j in range(1, width):
            total = total + weights[j] * window[i + width - 1 - j]
        out.append(total)
    return out


def lasting(micros):
    return pl.CostEstimate(flops=int(micros * 1.15e9), bytes_accessed=0, transcendentals=0)


def spread(row):
    return jnp.broadcast_to(row, (SUBS, row.shape[-1]))


def mr_kernel(halo_ref, x_ref, short_ref, filter_ref, out_ref, xf, ue, qs, of, ff):
    rows = x_ref.shape[1]
    sub = rows // SUBS
    taps = short_ref.shape[1]
    length = filter_ref.shape[0]
    for g in range(3):
        xf[g, :MR_HALO, :] = halo_ref[g].astype(jnp.float32)
        xf[g, MR_HALO:, :] = x_ref[g].astype(jnp.float32)
    ff[...] = filter_ref[...].astype(jnp.float32)
    weights = [[spread(short_ref[g, pl.ds(j, 1), :]) for j in range(taps)] for g in range(3)]

    def products(step, _):
        first = MR_HALO - sub + step * STEP
        keys = featurize(xf.at[1], weights[1], first, sub)
        values = featurize(xf.at[2], weights[2], first, sub)
        for i in range(STEP):
            ue[step * STEP + i] = (keys[i] * values[i]).astype(jnp.bfloat16).astype(jnp.float32)
        return 0

    lax.fori_loop(0, 2 * sub // STEP, products, 0)

    def queries(step, _):
        found = featurize(xf.at[0], weights[0], MR_HALO + step * STEP, sub)
        for i in range(STEP):
            qs[step * STEP + i] = found[i]
        return 0

    lax.fori_loop(0, sub // STEP, queries, 0)

    def conv(tile, _):
        base = tile * TILE

        def taps_of(part, acc):
            acc = list(acc)
            start = sub + base - part * TILE - (TILE - 1)
            window = [ue[start + m] for m in range(2 * TILE - 1)]
            for j in range(TILE):
                weight = spread(ff[pl.ds(part * TILE + j, 1), :])
                for i in range(TILE):
                    acc[i] = acc[i] + weight * window[i - j + TILE - 1]
            return tuple(acc)

        zero = jnp.zeros((SUBS, LANES), jnp.float32)
        acc = lax.fori_loop(0, length // TILE, taps_of, (zero,) * TILE)
        for i in range(TILE):
            of[pl.ds(base + i, SUBS, stride=sub), :] = acc[i] * qs[base + i]
        return 0

    lax.fori_loop(0, sub // TILE, conv, 0)
    out_ref[...] = of[...].astype(jnp.bfloat16)


def mr_operator(halo, x, short, filters, first, count):
    rows = x.shape[1]
    sub = rows // SUBS
    skip = first // LANES
    return pl.pallas_call(
        mr_kernel,
        grid=(count // LANES,),
        out_shape=jax.ShapeDtypeStruct((rows, count), jnp.bfloat16),
        in_specs=[
            pl.BlockSpec((3, MR_HALO, LANES), lambda i: (0, 0, i + skip)),
            pl.BlockSpec((3, rows, LANES), lambda i: (0, 0, i + skip)),
            pl.BlockSpec((3, short.shape[1], LANES), lambda i: (0, 0, i + skip)),
            pl.BlockSpec((filters.shape[0], LANES), lambda i: (0, i + skip)),
        ],
        out_specs=pl.BlockSpec((rows, LANES), lambda i: (0, i)),
        scratch_shapes=[
            pltpu.VMEM((3, MR_HALO + rows, LANES), jnp.float32),
            pltpu.VMEM((2 * sub, SUBS, LANES), jnp.float32),
            pltpu.VMEM((sub, SUBS, LANES), jnp.float32),
            pltpu.VMEM((rows, LANES), jnp.float32),
            pltpu.VMEM((filters.shape[0], LANES), jnp.float32),
        ],
        compiler_params=pltpu.CompilerParams(vmem_limit_bytes=24 * MIB),
        cost_estimate=lasting(rows * count * 6.8e-5),
        name="mr_operator",
    )(halo, x, short, filters)


def project(cols_ref, a_ref, blocks, pick):
    total = None
    for k, block in enumerate(blocks):
        w = pick(block)
        cols = a_ref[:, pl.ds(pl.multiple_of(cols_ref[k], LANES), w.shape[0])]
        part = jnp.dot(cols, w, preferred_element_type=jnp.float32)
        total = part if total is None else total + part
    return total


def stream_kernel(n_pieces, n_blocks, cols_ref, resid_ref, *refs):
    pieces = refs[:n_pieces]
    blocks = refs[n_pieces : n_pieces + n_blocks]
    out_ref, gated, sems = refs[n_pieces + n_blocks :]
    copies = []
    at = 0
    for i, piece in enumerate(pieces):
        width = piece.shape[1]
        copies.append(pltpu.make_async_copy(piece, gated.at[:, pl.ds(at, width)], sems.at[i]))
        at += width
    for copy in copies:
        copy.start()
    out_ref[:LR_HALO, :] = jnp.zeros((LR_HALO, out_ref.shape[1]), out_ref.dtype)
    for copy in copies:
        copy.wait()

    def tile(i, _):
        lanes = pl.ds(pl.multiple_of(i * CHUNK, CHUNK), CHUNK)
        projected = project(cols_ref, gated, blocks, lambda b: b[:, lanes])
        total = resid_ref[:, lanes].astype(jnp.float32) + projected
        out_ref[LR_HALO:, lanes] = total.astype(jnp.bfloat16)
        return 0

    lax.fori_loop(0, out_ref.shape[1] // CHUNK, tile, 0)


def stream_rows(cols, resid, pieces, blocks):
    rows, channels = resid.shape
    depth = sum(p.shape[1] for p in pieces)
    vmem = pl.BlockSpec(memory_space=pltpu.VMEM)
    return pl.pallas_call(
        functools.partial(stream_kernel, len(pieces), len(blocks)),
        out_shape=jax.ShapeDtypeStruct((LR_HALO + rows, channels), jnp.bfloat16),
        in_specs=[pl.BlockSpec(memory_space=pltpu.SMEM), vmem]
        + [pl.BlockSpec(memory_space=pl.ANY)] * len(pieces)
        + [vmem] * len(blocks),
        out_specs=vmem,
        scratch_shapes=[
            pltpu.VMEM((rows, depth), jnp.bfloat16),
            pltpu.SemaphoreType.DMA((len(pieces),)),
        ],
        compiler_params=pltpu.CompilerParams(vmem_limit_bytes=44 * MIB),
        cost_estimate=lasting(rows * channels * depth * 4e-9),
        name="stream_rows",
    )(cols, resid, *pieces, *blocks)


def norm_kernel(n_pieces, gain_ref, *refs):
    pieces, out_ref = refs[:n_pieces], refs[n_pieces]
    values = [p[...].astype(jnp.float32) for p in pieces]
    squares = sum(jnp.sum(v * v, axis=1, keepdims=True) for v in values)
    scale = lax.rsqrt(squares / out_ref.shape[1] + norm_eps)
    width = pieces[0].shape[1]
    for i, v in enumerate(values):
        lanes = slice(i * width, (i + 1) * width)
        out_ref[:, lanes] = (v * scale * gain_ref[:, lanes]).astype(jnp.bfloat16)


def norm_rows(gain, pieces):
    rows, width = pieces[0].shape
    depth = width * len(pieces)
    block = 80
    return pl.pallas_call(
        functools.partial(norm_kernel, len(pieces)),
        grid=(rows // block,),
        out_shape=jax.ShapeDtypeStruct((rows, depth), jnp.bfloat16),
        in_specs=[pl.BlockSpec((1, depth), lambda i: (0, 0))]
        + [pl.BlockSpec((block, width), lambda i: (i, 0))] * len(pieces),
        out_specs=pl.BlockSpec((block, depth), lambda i: (i, 0)),
        compiler_params=pltpu.CompilerParams(vmem_limit_bytes=24 * MIB),
        cost_estimate=lasting(rows * depth * 2.2e-6),
        name="norm_rows",
    )(gain, *pieces)


def shifted(value, steps):
    place = lax.broadcasted_iota(jnp.int32, value.shape, 0)
    return jnp.where(place >= steps, pltpu.roll(value, steps, 0), 0.0)


def lr_kernel(n_blocks, part, cols_ref, a_ref, short_ref, rate_ref, residue_ref, *refs):
    blocks = refs[:n_blocks]
    query_ref, local_ref, enter_ref, last_ref, xs, us = refs[n_blocks:]
    rows = a_ref.shape[0] - LR_HALO
    sub = rows // SUBS
    taps = short_ref.shape[1]
    states = rate_ref.shape[0]
    tiles = CHUNK // LANES

    def group(g, _):
        found = project(
            cols_ref, a_ref, blocks, lambda b: b[g, :, part * CHUNK : (part + 1) * CHUNK]
        )
        found = found.astype(jnp.bfloat16).astype(jnp.float32)
        for t in range(tiles):
            xs[g * tiles + t] = found[:, t * LANES : (t + 1) * LANES]
        return 0

    lax.fori_loop(0, 3, group, 0)
    for t in range(tiles):
        lanes = slice(t * LANES, (t + 1) * LANES)
        weights = [
            [spread(short_ref[g, pl.ds(j, 1), lanes]) for j in range(taps)] for g in range(3)
        ]

        def features(step, _):
            first = LR_HALO + step * STEP
            queries, keys, values = [
                featurize(xs.at[g * tiles + t], weights[g], first, sub) for g in range(3)
            ]
            for i in range(STEP):
                query_ref[step * STEP + i, :, lanes] = queries[i]
                us[step * STEP + i] = (keys[i] * values[i]).astype(jnp.bfloat16).astype(jnp.float32)
            return 0

        lax.fori_loop(0, sub // STEP, features, 0)
        rate = rate_ref[:, lanes]
        coef = residue_ref[:, lanes] * jnp.sqrt(2.0 * rate)
        decay = jnp.exp(-rate)
        decays = [spread(decay[n : n + 1]) for n in range(states)]
        coefs = [spread(coef[n : n + 1]) for n in range(states)]

        def advance(step, held):
            held = list(held)
            for i in range(4):
                u = us[step * 4 + i]
                terms = []
                for n in range(states):
                    held[n] = decays[n] * held[n] + u
                    terms.append(coefs[n] * held[n])
                while len(terms) > 1:
                    terms = [sum(terms[k : k + 2]) for k in range(0, len(terms), 2)]
                local_ref[step * 4 + i, :, lanes] = terms[0]
            return tuple(held)

        zero = jnp.zeros((SUBS, LANES), jnp.float32)
        held = lax.fori_loop(0, sub // 4, advance, (zero,) * states)
        for n in range(states):
            total = held[n]
            for steps in (1, 2, 4):
                total = total + spread(jnp.exp(-rate[n : n + 1] * (sub * steps))) * shifted(
                    total, steps
                )
            enter_ref[n, :, lanes] = shifted(total, 1)
            last_ref[n : n + 1, lanes] = total[SUBS - 1 : SUBS]


def lr_local(cols, a, short, rate, residue, blocks, first, part):
    rows = a.shape[0] - LR_HALO
    sub = rows // SUBS
    states = rate.shape[0]
    skip = first // CHUNK + part
    vmem = pl.BlockSpec(memory_space=pltpu.VMEM)
    depth = a.shape[1]
    return pl.pallas_call(
        functools.partial(lr_kernel, len(blocks), part),
        grid=(1,),
        out_shape=(
            jax.ShapeDtypeStruct((sub, SUBS, CHUNK), jnp.float32),
            jax.ShapeDtypeStruct((sub, SUBS, CHUNK), jnp.float32),
            jax.ShapeDtypeStruct((states, SUBS, CHUNK), jnp.float32),
            jax.ShapeDtypeStruct((states, CHUNK), jnp.float32),
        ),
        in_specs=[
            pl.BlockSpec(memory_space=pltpu.SMEM),
            vmem,
            pl.BlockSpec((3, short.shape[1], CHUNK), lambda i: (0, 0, skip)),
            pl.BlockSpec((states, CHUNK), lambda i: (0, skip)),
            pl.BlockSpec((states, CHUNK), lambda i: (0, skip)),
        ]
        + [vmem] * len(blocks),
        out_specs=(vmem, vmem, vmem, vmem),
        scratch_shapes=[
            pltpu.VMEM((3 * (CHUNK // LANES), LR_HALO + rows, LANES), jnp.float32),
            pltpu.VMEM((sub, SUBS, LANES), jnp.float32),
        ],
        compiler_params=pltpu.CompilerParams(vmem_limit_bytes=44 * MIB),
        cost_estimate=lasting(rows * CHUNK * depth * 1.7e-8),
        name="lr_local",
    )(cols, a, short, rate, residue, *blocks)


def finish_kernel(n_last, odd_ref, rate_ref, residue_ref, query_ref, local_ref, enter_ref, *refs):
    lasts = refs[:n_last]
    out_ref, of = refs[n_last:]
    sub = query_ref.shape[0]
    rate = rate_ref[...]
    states = rate.shape[0]
    coef = residue_ref[...] * jnp.sqrt(2.0 * rate)
    decay = jnp.exp(-rate)
    device = jnp.exp(-rate * (sub * SUBS))
    incoming = lasts[n_last - 1][...]
    for k in reversed(range(1, n_last - 1)):
        incoming = incoming * (device * device) + lasts[k][...]
    incoming = jnp.where(odd_ref[0] == 1, incoming * device + lasts[0][...], incoming)
    place = lax.broadcasted_iota(jnp.int32, (SUBS, LANES), 0).astype(jnp.float32) * float(sub)
    decays = [spread(decay[n : n + 1]) for n in range(states)]
    held = []
    for n in range(states):
        entering = enter_ref[n] + jnp.exp(-rate[n : n + 1] * place) * incoming[n : n + 1]
        held.append(coef[n : n + 1] * entering)

    def advance(step, held):
        held = list(held)
        for i in range(4):
            r = step * 4 + i
            for n in range(states):
                held[n] = decays[n] * held[n]
            terms = held
            while len(terms) > 1:
                terms = [sum(terms[k : k + 2]) for k in range(0, len(terms), 2)]
            of[pl.ds(r, SUBS, stride=sub), :] = query_ref[r] * (local_ref[r] + terms[0])
        return tuple(held)

    lax.fori_loop(0, sub // 4, advance, tuple(held))
    out_ref[...] = of[...].astype(jnp.bfloat16)


def lr_finish(odd, rate, residue, query, local, enter, lasts, first, part):
    sub = query.shape[0]
    states = rate.shape[0]
    past = part * (CHUNK // LANES)
    skip = first // LANES + past
    return pl.pallas_call(
        functools.partial(finish_kernel, len(lasts)),
        grid=(CHUNK // LANES,),
        out_shape=jax.ShapeDtypeStruct((sub * SUBS, CHUNK), jnp.bfloat16),
        in_specs=[
            pl.BlockSpec(memory_space=pltpu.SMEM),
            pl.BlockSpec((states, LANES), lambda i: (0, i + skip)),
            pl.BlockSpec((states, LANES), lambda i: (0, i + skip)),
            pl.BlockSpec((sub, SUBS, LANES), lambda i: (0, 0, i)),
            pl.BlockSpec((sub, SUBS, LANES), lambda i: (0, 0, i)),
            pl.BlockSpec((states, SUBS, LANES), lambda i: (0, 0, i)),
        ]
        + [pl.BlockSpec((states, LANES), lambda i: (0, i + past))] * len(lasts),
        out_specs=pl.BlockSpec((sub * SUBS, LANES), lambda i: (0, i)),
        scratch_shapes=[pltpu.VMEM((sub * SUBS, LANES), jnp.float32)],
        compiler_params=pltpu.CompilerParams(vmem_limit_bytes=24 * MIB),
        cost_estimate=lasting(sub * SUBS * CHUNK * 8e-6),
        name="lr_finish",
    )(odd, rate, residue, query, local, enter, *lasts)


def after(values, ties):
    if not ties:
        return values
    return lax.optimization_barrier((values, ties))[0]


class Ring:
    def __init__(self, own, order):
        count = len(order)
        self.steps = count // 2
        self.right = [(order[i], order[(i + 1) % count]) for i in range(count)]
        self.left = [(b, a) for a, b in self.right]
        self.ahead, self.behind = [own], [own]

    def step(self, ties):
        k = len(self.ahead)
        a, b = self.ahead[-1], self.behind[-1]
        if k == self.steps:
            half = a.shape[-2] // 2
            a, b = a[..., :half, :], b[..., half:, :]
        a, b = after((a, b), ties)
        self.ahead.append(lax.ppermute(a, "seq", self.right))
        self.behind.append(lax.ppermute(b, "seq", self.left))
        return (self.ahead[-1], self.behind[-1])

    def blocks(self):
        return self.ahead + self.behind[1:]


def block_columns(order, depth, channels):
    count = len(order)
    block = depth // count
    place = lax.axis_index("seq")
    spot = jnp.asarray([order.index(i) for i in range(count)], jnp.int32)[place]
    table = jnp.asarray(order, jnp.int32)
    half = count // 2
    turns = list(range(half + 1)) + [-k for k in range(1, half + 1)]
    source = table[(spot - jnp.asarray(turns, jnp.int32)) % count]
    shift = jnp.asarray([0] * (2 * half) + [block // 2], jnp.int32)
    row = source * block + shift
    peer = jnp.bitwise_xor(row // channels, lax.axis_index("tp"))
    return peer * channels + row % channels


def swap_tp(value, mask):
    count = lax.axis_size("tp")
    return lax.ppermute(value, "tp", [(i, i ^ mask) for i in range(count)])


def tp_pieces(own, count, ties):
    pieces = [own, swap_tp(own, 1)]
    for mask in range(2, count, 2):
        far = swap_tp(own, mask)
        pieces += [far, swap_tp(after(far, ties), 1)]
    return pieces


def from_behind(value, steps):
    count = lax.axis_size("seq")
    return lax.ppermute(value, "seq", [(i, i + steps) for i in range(count - steps)])


def earlier_states(last, rate, rows):
    count = lax.axis_size("seq")
    odd = lax.rem(lax.axis_index("seq"), 2)
    other = lax.ppermute(last, "seq", [(i, i ^ 1) for i in range(count)])
    first, second = jnp.where(odd == 1, other, last), jnp.where(odd == 1, last, other)
    both = first * jnp.exp(-rate * rows) + second
    return odd.reshape(1), other, [from_behind(both, 2 * k) for k in range(1, count // 2)]


def per_device(
    mr_qkv,
    residual_in,
    mr_short,
    mr_filter,
    mr_out,
    norm_gain,
    lr_in,
    lr_short,
    lr_rate,
    lr_residue,
):
    rows, _, channels = mr_qkv.shape
    n_seq, n_tp = lax.axis_size("seq"), lax.axis_size("tp")
    depth = channels * n_tp
    order = ring_order(n_seq)
    x = mr_qkv.transpose(1, 0, 2)
    short = mr_short.transpose(1, 0, 2)
    halo = from_behind(x[:, rows - MR_HALO :], 1)
    starts = list(range(0, channels, CHUNK))
    final = len(starts)
    wide = [2 * CHUNK] * (channels >= 4 * CHUNK)
    wide += [CHUNK] * ((channels - sum(wide)) // CHUNK)

    rings = [Ring(mr_out, order)]
    weights = lr_in.transpose(1, 0, 2)
    first = 0
    for width in wide:
        rings.append(Ring(weights[:, :, first : first + width], order))
        first += width
    steps = rings[0].steps
    begins = [0] + [steps - 1 + i * (steps - 2) for i in range(len(wide))]
    plan = [
        [(i, turn - begin) for i, begin in enumerate(begins) if 0 <= turn - begin < steps]
        for turn in range(begins[-1] + steps)
    ]
    turns = len(plan)
    waits = {}
    done = []

    def drive(turn):
        while len(done) < min(turn, turns):
            now = len(done)
            ties = tuple(waits.get(now, ()))
            got = []
            for i, k in plan[now]:
                fresh = k == 0 and now > 0
                got += rings[i].step(ties + (tuple(done[-1][:2]) if fresh else ()))
            done.append(got)
        return tuple(done[min(turn, turns) - 1]) if turn > 0 else ()

    def hold(turn, value):
        waits.setdefault(turn + 1, []).append(value)

    waits[0] = [halo]
    parts, near, far, passed = [], [], [], []
    for i, first in enumerate(starts):
        ties = drive(i)
        if i >= 2:
            ties += tuple(far[i - 2])
        if i >= 3:
            ties += tuple(passed[i - 3])
        parts.append(mr_operator(halo, x, after(short, ties), mr_filter, first, CHUNK))
        hold(i, parts[-1])
        if i > 0:
            passed.append([swap_tp(after(f, [parts[i]]), 1) for f in far[i - 1]])
        part = parts[-1] if i < final - 1 else after(parts[-1], drive(steps)[:2])
        near.append(swap_tp(parts[-1], 1))
        far.append([swap_tp(part, mask) for mask in range(2, n_tp, 2)])
    passed.append([swap_tp(f, 1) for f in far[-1]])
    pieces = []
    for m in range(n_tp):
        for i in range(final):
            if m < 2:
                pieces.append((parts, near)[m][i])
            else:
                pieces.append((far, passed)[m % 2][i][m // 2 - 1])
    cols = after(block_columns(order, depth, channels), drive(steps))
    extended = stream_rows(cols, residual_in, pieces, rings[0].blocks())
    stream = extended[LR_HALO:]
    rim = from_behind(extended[rows:], 1)
    extended = lax.dynamic_update_slice(extended, rim, (0, 0))
    gains = norm_gain.reshape(n_tp, channels)
    peers = jnp.bitwise_xor(jnp.arange(n_tp, dtype=jnp.int32), lax.axis_index("tp"))
    gain = jnp.take(gains, peers, axis=0).reshape(1, depth)
    shared = tp_pieces(extended, n_tp, drive(steps + 1))
    turn = steps + 2
    normed = norm_rows(after(gain, drive(turn)), shared)
    hold(turn, normed)

    lr_taps = lr_short.transpose(1, 0, 2)
    found = []
    first = 0
    for i, width in enumerate(wide):
        turn = begins[i + 1] + steps - 1
        drive(turn + 1)
        taps = lr_taps
        for part in range(width // CHUNK):
            if part > 0:
                taps = after(lr_taps, drive(turn + 2))
            found.append(
                lr_local(cols, normed, taps, lr_rate, lr_residue, rings[i + 1].blocks(), first, part)
            )
            hold(turn + 1 + part, found[-1][3])
        first += width
    odd, other, fars = earlier_states(
        jnp.concatenate([f[3] for f in found], axis=1), lr_rate, rows
    )
    outs = [
        lr_finish(odd, lr_rate, lr_residue, query, local, enter, [other] + fars, 0, part)
        for part, (query, local, enter, _) in enumerate(found)
    ]
    return (stream, jnp.concatenate(outs, axis=1))


def solution(mesh):
    placed = (
        P("seq", None, "tp"),
        P("seq", "tp"),
        P(None, None, "tp"),
        P(None, "tp"),
        P("seq", "tp"),
        P(),
        P("seq", None, "tp"),
        P(None, None, "tp"),
        P(None, "tp"),
        P(None, "tp"),
    )
    return jax.shard_map(
        per_device,
        mesh=mesh,
        in_specs=placed,
        out_specs=(P("seq", "tp"), P("seq", "tp")),
        check_vma=False,
    )
```
